512 devices in a mesh: ctx: 64 (over y, z_lo, x), ch: 8 (over z_hi, core).
Axes of the slice: x: 4, y: 8, z: 8 (z_hi: 4, z_lo: 2; z = z_hi * 2 + z_lo), core: 2. Of those that a mesh axis runs over, the one named last changes fastest.
Arguments:
- layer_input: bfloat16 [1280, 32768], P('ch', 'ctx'), may hold values from -6 to 6
- w_block: bfloat16 [512, 512], replicated, may hold values from -0.25 to 0.25
- w_cross: bfloat16 [64, 64], replicated, may hold values from -0.75 to 0.75
- ch_first: bfloat16 [8, 160, 160], P('ch'), may hold values from -0.5 to 0.5
- ch_second: bfloat16 [160, 8, 8], P('ch'), may hold values from -2 to 2
- gate_gain: float32 [1280], P('ch'), may hold values from 0.5 to 2
- gate_bias: float32 [1280], P('ch'), may hold values from -3 to 3
- cotangent: bfloat16 [1280, 32768], P('ch', 'ctx'), may hold values from -6 to 6
Outputs:
- output: bfloat16 [1280, 32768], P('ch', 'ctx')
- grad_input: bfloat16 [1280, 32768], P('ch', 'ctx')
- grad_block: float32 [512, 512], replicated
- grad_cross: float32 [64, 64], replicated
- grad_first: float32 [8, 160, 160], P('ch')
- grad_second: float32 [160, 8, 8], P('ch')
- grad_gain: float32 [1280], P('ch')
- grad_bias: float32 [1280], P('ch')
The draws below stay inside these ranges and needn't reach their ends.
All inputs are finite; a program needn't handle non-finite values.
Results may differ from the reference program's by a relative error of at most 0.007.
Values may be sent and summed in bfloat16 or wider, within the bound.
No kernel may reach another device: no remote copies, remote signals or barrier semaphores. Data moves between devices by JAX's collectives and lax.ppermute only.
A program may use at most 64 MiB of HBM per device.

```python
import jax
import jax.numpy as jnp
from jax import lax

BLK = 512
CB = 8
CS = 160
D = 1280
L = 32768
NB = 64


def block_levels(rng, extent, shards, low, largest):
    factor_of = 1.0
    for axis_at, shards_of in shards:
        steps = jax.random.uniform(jax.random.fold_in(jax.random.fold_in(rng, 6), axis_at), (shards_of,), jnp.float32, low / len(shards), largest / len(shards))
        factor_of = factor_of * jnp.repeat(jnp.exp(steps), extent[axis_at] // shards_of).reshape((-1,) + (1,) * (len(extent) - 1 - axis_at))
    return factor_of


def centred(key, extent, width, reach, shards=(), kind=jnp.bfloat16):
    level = block_levels(key, extent, shards, -0.22, 0.18) if shards else 1.0
    array = jax.random.normal(key, extent, jnp.float32) * width * level
    return jnp.minimum(jnp.maximum(array, -reach), reach).astype(kind)


def setup_inputs(seed: int = 0) -> dict:
    key_list = jax.random.split(jax.random.key(seed), 9)
    layer_input = centred(key_list[0], (D, L), 1.0, 6.0, ((0, 8), (1, 64)))
    w_block = centred(key_list[1], (BLK, BLK), BLK ** -0.5, 0.25)
    w_cross = centred(key_list[2], (NB, NB), NB ** -0.5, 0.75)
    ch_first = centred(key_list[3], (CB, CS, CS), CS ** -0.5, 0.5, ((0, 8),))
    ch_second = centred(key_list[4], (CS, CB, CB), CB ** -0.5, 2.0, ((0, 8),))
    gate_gain = jnp.clip(0.5 + 1.5 * jax.random.uniform(key_list[5], (D,), jnp.float32) ** block_levels(key_list[5], (D,), ((0, 8),), -0.2, 0.2), 0.5, 2.0)
    gate_bias = centred(key_list[6], (D,), 1.0, 3.0, ((0, 8),), jnp.float32)
    cotangent = centred(key_list[7], (D, L), 1.0, 6.0, ((0, 8), (1, 64)))
    return dict(layer_input=layer_input, w_block=w_block, w_cross=w_cross, ch_first=ch_first, ch_second=ch_second, gate_gain=gate_gain, gate_bias=gate_bias, cotangent=cotangent)


def reference(layer_input, w_block, w_cross, ch_first, ch_second, gate_gain, gate_bias, cotangent):
    block_full = w_block.astype(jnp.float32)
    between_tiles_finished = w_cross.astype(jnp.float32)
    input_split = layer_input.reshape(CB, CS, NB, BLK)

    def seq_forward(input_part):
        first_factor_piece = jnp.einsum('cij,jk->cik', input_part.astype(jnp.float32), block_full).astype(jnp.bfloat16)
        mixed_sequence_piece = jnp.einsum('tdw,dx->txw', first_factor_piece.astype(jnp.float32), between_tiles_finished).astype(jnp.bfloat16)
        return (first_factor_piece, mixed_sequence_piece)
    first_all, mixed_all = lax.map(seq_forward, input_split)
    mixed_seq = mixed_all.reshape(D, L)
    input_full = layer_input.astype(jnp.float32)
    gate_value = jax.nn.sigmoid(input_full * gate_gain[:, None] + gate_bias[:, None])
    hidden = (input_full + gate_value * mixed_seq.astype(jnp.float32)).astype(jnp.bfloat16)
    hidden_grouped = hidden.reshape(CB, CS, L)
    pre_act = jnp.einsum('gkm,gmn->gkn', ch_first.astype(jnp.float32), hidden_grouped.astype(jnp.float32))
    activated = jax.nn.gelu(pre_act).astype(jnp.bfloat16)
    path_choice_flag = jnp.einsum('kgh,hkn->gkn', ch_second.astype(jnp.float32), activated.astype(jnp.float32)).astype(jnp.bfloat16)
    output = (hidden_grouped.astype(jnp.float32) + path_choice_flag.astype(jnp.float32)).astype(jnp.bfloat16).reshape(D, L)
    cot_grouped = cotangent.astype(jnp.float32).reshape(CB, CS, L)
    d_act = jnp.einsum('kgh,gkn->hkn', ch_second.astype(jnp.float32), cot_grouped).astype(jnp.bfloat16)
    grad_second = jnp.einsum('gkn,hkn->kgh', cot_grouped, activated.astype(jnp.float32))
    gelu_pull = jax.vjp(jax.nn.gelu, pre_act)[1]
    d_pre = gelu_pull(d_act.astype(jnp.float32))[0].astype(jnp.bfloat16)
    grad_first = jnp.einsum('gkn,gmn->gkm', d_pre.astype(jnp.float32), hidden_grouped.astype(jnp.float32))
    d_hidden = cot_grouped + jnp.einsum('gkm,gkn->gmn', ch_first.astype(jnp.float32), d_pre.astype(jnp.float32))
    d_hidden = d_hidden.reshape(D, L)
    d_mixed = (d_hidden * gate_value).astype(jnp.bfloat16)
    d_gate = d_hidden * mixed_seq.astype(jnp.float32) * gate_value * (1.0 - gate_value)
    grad_gain = lax.optimization_barrier(jnp.sum(d_gate * input_full, axis=1))
    grad_bias = lax.optimization_barrier(jnp.sum(d_gate, axis=1))

    def seq_back(totals, pieces):
        input_part, first_factor_piece, blended_deriv_share = pieces
        leading_matrix_deriv = jnp.einsum('fzq,bz->fbq', blended_deriv_share.astype(jnp.float32), between_tiles_finished).astype(jnp.bfloat16)
        cross_block_increment = jnp.einsum('jfp,jop->fo', first_factor_piece.astype(jnp.float32), blended_deriv_share.astype(jnp.float32))
        block_add = jnp.einsum('cij,cik->jk', input_part.astype(jnp.float32), leading_matrix_deriv.astype(jnp.float32))
        d_input = jnp.einsum('cik,jk->cij', leading_matrix_deriv.astype(jnp.float32), block_full)
        return ((totals[0] + block_add, totals[1] + cross_block_increment), d_input)
    zero_sums = (jnp.zeros((BLK, BLK), jnp.float32), jnp.zeros((NB, NB), jnp.float32))
    weight_grads, d_input_all = lax.scan(seq_back, zero_sums, (input_split, first_all, d_mixed.reshape(CB, CS, NB, BLK)))
    grad_input = (d_hidden + d_gate * gate_gain[:, None] + d_input_all.reshape(D, L)).astype(jnp.bfloat16)
    return (output, grad_input, weight_grads[0], weight_grads[1], grad_first, grad_second, grad_gain, grad_bias)
```

```python
import functools

import jax
import jax.numpy as jnp
from jax import lax
from jax.experimental import pallas as pl
from jax.experimental.pallas import tpu as pltpu
from jax.sharding import PartitionSpec as P

BF = jnp.bfloat16
F32 = jnp.float32
NB = 64
BLK = 512
CB = 8
CS = 160
KCH = 20
W = 256
HALF = 128
TOK = 64


def dot(a, b, dims=((1,), (0,))):
    return lax.dot_general(a, b, (dims, ((), ())), preferred_element_type=F32)


NN = ((1,), (0,))
NT = ((1,), (1,))
TN = ((0,), (0,))


def iota(shape, axis):
    return lax.broadcasted_iota(jnp.int32, shape, axis)


def ones_where(cond):
    return jnp.where(cond, 1.0, 0.0).astype(BF)


def lanes_of(x):
    groups = x.shape[0] // 8
    left = x[:, :HALF].reshape(groups, 8, HALF)
    right = x[:, HALF:].reshape(groups, 8, HALF)
    return left, right


def call(body, out_shapes, *args, scratch=(), smem=()):
    specs = [
        pl.BlockSpec(memory_space=pltpu.SMEM if at in smem else pltpu.VMEM)
        for at in range(len(args))
    ]
    return pl.pallas_call(
        body,
        out_shape=[jax.ShapeDtypeStruct(s, d) for s, d in out_shapes],
        in_specs=specs,
        out_specs=[pl.BlockSpec(memory_space=pltpu.VMEM) for _ in out_shapes],
        scratch_shapes=list(scratch),
        compiler_params=pltpu.CompilerParams(vmem_limit_bytes=48 * 1024 * 1024),
    )(*args)


def prepare(x_ref, cot_ref, second_ref, first_ref, gain_ref, bias_ref, cross_ref,
            xt_ref, cott_ref, weight_ref, scale_ref, kron_ref, kront_ref, pad_ref):
    zeros = jnp.zeros((W - CS, BLK), F32)
    xt = jnp.concatenate([x_ref[...].astype(F32), zeros], axis=0).T
    xt_ref[...] = xt.reshape(NB, 8, W).astype(BF)
    cott = jnp.concatenate([cot_ref[...].astype(F32), zeros], axis=0).T
    place = ones_where(iota((KCH, W), 1) == iota((KCH, W), 0) + CS)
    factor = dot(second_ref[...], place, TN)
    cott_ref[...] = (cott.reshape(CB, TOK, W) + factor[None]).astype(BF)
    pad_ref[...] = jnp.zeros((W, W), F32)
    pad_ref[:CS, :CS] = first_ref[0].astype(F32)
    weight_ref[...] = pad_ref[...].astype(BF)
    scale_ref[...] = jnp.zeros((8, W), F32)
    scale_ref[0:1, :CS] = gain_ref[...]
    scale_ref[1:2, :CS] = bias_ref[...]
    spread = ones_where(iota((BLK, NB), 0) // 8 == iota((BLK, NB), 1))
    same = iota((BLK, BLK), 0) % 8 == iota((BLK, BLK), 1) % 8
    half = dot(spread, cross_ref[...], NN).astype(BF)
    kron_ref[...] = jnp.where(same, dot(half, spread, NT), 0.0).astype(BF)
    half = dot(spread, cross_ref[...], NT).astype(BF)
    kront_ref[...] = jnp.where(same, dot(half, spread, NT), 0.0).astype(BF)


def cross_forward(kront_ref, cols_ref, out_ref):
    cols = cols_ref[...].astype(F32).reshape(BLK, W).astype(BF)
    out_ref[...] = dot(kront_ref[...], cols).reshape(NB, 8, W).astype(BF)


def channel_forward(u_ref, block_ref, xt_ref, scale_ref, weight_ref, cot_ref,
                    send_ref, mixed_ref, gate_ref, hidden_ref, slope_ref, second_ref):
    u = u_ref[...].astype(F32).reshape(BLK, W).astype(BF)
    mixed = dot(block_ref[...], u, TN).astype(BF)
    mixed_ref[...] = mixed
    xt = xt_ref[...].astype(F32).reshape(BLK, W)
    gate = jax.nn.sigmoid(xt * scale_ref[0:1, :] + scale_ref[1:2, :])
    gate_ref[...] = gate
    hidden = (xt + gate * mixed.astype(F32)).astype(BF)
    hidden_ref[...] = hidden
    pre = dot(hidden, weight_ref[...], NT)
    root = 0.7978845608028654
    square = pre * pre
    curve = jnp.tanh(root * (pre + 0.044715 * (square * pre)))
    act = pre * (0.5 * (1.0 + curve))
    slope_ref[...] = 0.5 * (1.0 + curve) + pre * (0.5 * (1.0 - curve * curve)) * (
        root * (1.0 + (3 * 0.044715) * square)
    )
    send_ref[:, :TOK, :] = act.astype(BF).reshape(CB, TOK, W)
    second = jnp.zeros((TOK, W), F32)
    for g in range(CB):
        pick = (iota((W, W), 0) >= CS) & (iota((W, W), 1) == iota((W, W), 0) - CS + KCH * g)
        pick = pick & (iota((W, W), 0) < CS + KCH)
        second = second + dot(cot_ref[g], ones_where(pick))
    second_ref[...] = second
    inside = iota((TOK, W), 1) < CS
    for g2 in range(CB):
        total = jnp.zeros((TOK, W), F32)
        for g in range(CB):
            total = total + second[g * CB + g2][None, :] * cot_ref[g].astype(F32)
        send_ref[g2, TOK:, :] = jnp.where(inside, total, 0.0).astype(BF)


def channel_backward(recv_ref, cot_ref, cott_ref, second_ref, mixed_ref, gate_ref, hidden_ref,
                     slope_ref, weight_ref, xt_ref, scale_ref, block_ref, u_ref,
                     send_ref, branch_ref, rest_ref, misc_ref):
    second = second_ref[...]
    for g in range(CB):
        total = jnp.zeros((TOK, W), F32)
        for g2 in range(CB):
            total = total + second[g * CB + g2][None, :] * recv_ref[g2, :TOK, :].astype(F32)
        branch_ref[g] = total.astype(BF)
    misc_ref[...] = jnp.zeros(misc_ref.shape, F32)
    for g in range(CB):
        cot = cot_ref[g].astype(F32)
        for g2 in range(CB):
            row = 320 + g * CB + g2
            misc_ref[row:row + 1, :] = jnp.sum(
                cot * recv_ref[g2, :TOK, :].astype(F32), axis=0, keepdims=True
            )
    d_act = recv_ref[:, TOK:, :].reshape(BLK, W).astype(F32)
    d_pre = (d_act * slope_ref[...]).astype(BF)
    hidden = hidden_ref[...]
    grad_first = dot(d_pre, hidden, TN)
    misc_ref[0:CS, :] = grad_first[:CS]
    inside = iota((BLK, W), 1) < CS
    cot = jnp.where(inside, cott_ref[...].reshape(BLK, W).astype(F32), 0.0)
    d_hidden = cot + dot(d_pre, weight_ref[...], NN)
    gate = gate_ref[...]
    d_mixed = (d_hidden * gate).astype(BF)
    d_gate = d_hidden * mixed_ref[...].astype(F32) * gate * (1.0 - gate)
    xt = xt_ref[...].astype(F32).reshape(BLK, W)
    misc_ref[448:449, :] = jnp.sum(d_gate * xt, axis=0, keepdims=True)
    misc_ref[449:450, :] = jnp.sum(d_gate, axis=0, keepdims=True)
    rest_ref[...] = d_hidden + d_gate * scale_ref[0:1, :]
    v = dot(block_ref[...], d_mixed, NN)
    u = u_ref[...].astype(F32).reshape(BLK, W).astype(BF)
    at = iota((CS, HALF), 1)

    def packed(x):
        keep = at[: x.shape[0]]
        left, right = x[:, :HALF], x[:, HALF:]
        first = jnp.where(keep >= 32, left, 0.0)
        moved = jnp.where(keep < 64, pltpu.roll(left, 32, 1), pltpu.roll(right, 64, 1))
        second = jnp.where((keep >= 32) & (keep < 96), moved, 0.0)
        return first, second

    first_a, first_b = packed(misc_ref[0:CS, :])
    second_a, second_b = packed(misc_ref[320:384, :])
    scale_a, scale_b = packed(misc_ref[448:456, :])
    misc = jnp.concatenate(
        [first_a, first_b, second_a, second_b, scale_a, scale_b, jnp.zeros((48, HALF), F32)], axis=0
    )
    left = v[:, :HALF].reshape(NB, 8, HALF)
    right = (jnp.where(iota((BLK, HALF), 1) < 32, v[:, HALF:], misc)).reshape(NB, 8, HALF)
    send_ref[:, 0:16, :] = jnp.concatenate([left, right], axis=1).astype(BF)
    d_block = dot(u, d_mixed, NT)
    parts = [d_block[:, HALF * s:HALF * (s + 1)].reshape(NB, 8, HALF) for s in range(4)]
    send_ref[:, 16:48, :] = jnp.concatenate(parts, axis=1).astype(BF)


def cross_backward(recv_ref, x_ref, kron_ref, branch_ref, send_ref, d_input_ref, misc_ref):
    head = recv_ref[:, 0:16, :].astype(F32)
    low = iota((NB, 8, HALF), 2) < 32
    left, right = head[:, 0:8, :], head[:, 8:16, :]
    v = jnp.concatenate(
        [left.reshape(BLK, HALF), jnp.where(low, right, 0.0).reshape(BLK, HALF)], axis=1
    ).astype(BF)
    misc_ref[...] = jnp.sum(right, axis=0)
    d_input_ref[...] = dot(kron_ref[...], v).astype(BF)
    x = x_ref[...].astype(F32).reshape(BLK, W).astype(BF)
    pairs = dot(x, v, NT)
    same = iota((BLK, BLK), 0) % 8 == iota((BLK, BLK), 1) % 8
    rows = jnp.sum(jnp.where(same, pairs, 0.0).reshape(NB, 8, BLK), axis=1)
    gather = ones_where(iota((BLK, HALF), 0) // 8 == iota((BLK, HALF), 1) - 64)
    high = rows.astype(BF)
    cross = dot(high, gather) + dot((rows - high.astype(F32)).astype(BF), gather)
    tail = jnp.sum(recv_ref[:, 16:48, :].astype(F32), axis=0)
    extra = jnp.concatenate([tail, misc_ref[...], jnp.zeros((8, HALF), F32)], axis=0).astype(BF)
    lane = iota((TOK, HALF), 1)
    for g in range(CB):
        branch = branch_ref[g].astype(F32)
        send_ref[g, 0:64, :] = branch[:, :HALF].astype(BF)
        send_ref[g, 64:128, :] = jnp.where(lane < 32, branch[:, HALF:], cross).astype(BF)
        send_ref[g, 128:176, :] = extra


def finish_output(recv_ref, hidden_ref, d_input_ref, misc_ref, flag_ref, out_ref, send_ref):
    low = iota((CB, TOK, HALF), 2) < 32
    right = recv_ref[:, 64:128, :].astype(F32)
    left = recv_ref[:, 0:64, :].astype(F32)
    branch = jnp.concatenate(
        [left.reshape(BLK, HALF), jnp.where(low, right, 0.0).reshape(BLK, HALF)], axis=1
    )
    total = hidden_ref[...].astype(F32) + branch
    out_ref[...] = total.T[:CS].astype(BF)
    cross = jnp.sum(right, axis=0)
    lane = iota((32, HALF), 1)
    cross = jnp.where(lane < 64, pltpu.roll(cross[0:32], 64, 1), cross[32:64])
    block = jnp.sum(recv_ref[:, 128:160, :].astype(F32), axis=0)
    summed = jnp.sum(recv_ref[:, 160:176, :].astype(F32), axis=0)[0:8]
    misc = jnp.where(flag_ref[0] > 0, summed, misc_ref[...])
    d_input = d_input_ref[...].astype(F32)
    left = d_input[:, :HALF].reshape(NB, 8, HALF)
    right = jnp.where(
        iota((NB, 8, HALF), 2) < 32, d_input[:, HALF:].reshape(NB, 8, HALF), misc[None]
    )
    send_ref[:, 0:16, :] = jnp.concatenate([left, right], axis=1).astype(BF)
    tail = jnp.concatenate([block, cross], axis=0).astype(BF)
    send_ref[:, 16:80, :] = jnp.broadcast_to(tail[None], (NB, 64, HALF))


def finish(recv_ref, rest_ref, flag_ref, grad_ref, block_ref, cross_ref, first_ref, second_ref,
           gain_ref, bias_ref):
    head = recv_ref[:, 0:16, :].astype(F32)
    left, right = head[:, 0:8, :], head[:, 8:16, :].reshape(BLK, HALF)
    low = iota((BLK, HALF), 1) < 32
    d_input = jnp.concatenate([left.reshape(BLK, HALF), jnp.where(low, right, 0.0)], axis=1)
    grad_ref[...] = (rest_ref[...] + d_input).T[:CS].astype(BF)
    block = recv_ref[:, 16:48, :].astype(F32)
    for s in range(4):
        block_ref[:, HALF * s:HALF * (s + 1)] = block[:, 8 * s:8 * s + 8, :].reshape(BLK, HALF)
    cross = jnp.sum(recv_ref[:, 48:80, :].astype(F32), axis=0)
    cross_ref[0:32, :] = cross[:, 0:64]
    cross_ref[32:64, :] = pltpu.roll(cross, 64, 1)[:, 0:64]
    misc = right

    def unpacked(start, rows):
        a, b = misc[start:start + rows], misc[start + rows:start + 2 * rows]
        keep = iota((rows, HALF), 1)
        left = jnp.where(keep >= 32, a, pltpu.roll(b, 96, 1))
        return left, pltpu.roll(b, 64, 1)

    left, right = unpacked(0, CS)
    first_ref[0, :, 0:HALF] = left
    first_ref[0, :, HALF:CS] = right[:, 0:32]
    left, right = unpacked(320, 64)
    own = flag_ref[1] * KCH
    pick_left = ones_where(iota((KCH, HALF), 1) == iota((KCH, HALF), 0) + own)
    pick_right = ones_where(iota((KCH, HALF), 1) + HALF == iota((KCH, HALF), 0) + own)
    pick_right = jnp.where(iota((KCH, HALF), 1) < 32, pick_right, 0.0).astype(BF)
    second_ref[...] = dot(pick_left, left.astype(BF), NT) + dot(pick_right, right.astype(BF), NT)
    left, right = unpacked(448, 8)
    gain_ref[:, 0:HALF] = left[0:1]
    gain_ref[:, HALF:CS] = right[0:1, 0:32]
    bias_ref[:, 0:HALF] = left[1:2]
    bias_ref[:, HALF:CS] = right[1:2, 0:32]


def on_device(layer_input, w_block, w_cross, ch_first, ch_second, gate_gain, gate_bias, cotangent):
    swap = functools.partial(lax.all_to_all, split_axis=0, concat_axis=0, tiled=True)
    ctx, ch = lax.axis_index("ctx"), lax.axis_index("ch")
    flag = jnp.stack([((ctx >= 40) & (ctx < 56)).astype(jnp.int32), ch.astype(jnp.int32)])
    xt, cott, weight, scale, kron, kront = call(
        prepare,
        [((NB, 8, W), BF), ((CB, TOK, W), BF), ((W, W), BF), ((8, W), F32),
         ((BLK, BLK), BF), ((BLK, BLK), BF)],
        layer_input, cotangent, ch_second.reshape(KCH, CB * CB), ch_first,
        gate_gain.reshape(1, CS), gate_bias.reshape(1, CS), w_cross,
        scratch=[pltpu.VMEM((W, W), F32)],
    )
    x_cols = swap(xt, "ctx")
    cot_cols = swap(cott, "ch")
    (u_cols,) = call(cross_forward, [((NB, 8, W), BF)], kront, x_cols)
    u = swap(u_cols, "ctx")
    send, mixed, gate, hidden, slope, second = call(
        channel_forward,
        [((CB, 2 * TOK, W), BF), ((BLK, W), BF), ((BLK, W), F32), ((BLK, W), BF), ((BLK, W), F32),
         ((TOK, W), F32)],
        u, w_block, xt, scale, weight, cot_cols,
    )
    recv = swap(send, "ch")
    send, branch, rest = call(
        channel_backward,
        [((NB, 48, HALF), BF), ((CB, TOK, W), BF), ((BLK, W), F32)],
        recv, cot_cols, cott, second, mixed, gate, hidden, slope, weight, xt, scale, w_block, u,
        scratch=[pltpu.VMEM((456, W), F32)],
    )
    recv = swap(send, "ctx")
    send, d_input, misc = call(
        cross_backward,
        [((CB, 176, HALF), BF), ((BLK, W), BF), ((8, HALF), F32)],
        recv, x_cols, kron, branch,
    )
    recv = swap(send, "ch")
    output, send = call(
        finish_output,
        [((CS, BLK), BF), ((NB, 80, HALF), BF)],
        recv, hidden, d_input, misc, flag,
        smem=(4,),
    )
    recv = swap(send, "ctx")
    grad_input, grad_block, grad_cross, grad_first, grad_second, grad_gain, grad_bias = call(
        finish,
        [((CS, BLK), BF), ((BLK, BLK), F32), ((NB, NB), F32), ((1, CS, CS), F32),
         ((KCH, CB * CB), F32), ((1, CS), F32), ((1, CS), F32)],
        recv, rest, flag,
        smem=(2,),
    )
    return (
        output,
        grad_input,
        grad_block,
        grad_cross,
        grad_first,
        grad_second.reshape(KCH, CB, CB),
        grad_gain.reshape(CS),
        grad_bias.reshape(CS),
    )


def solution(mesh):
    in_specs = (
        P("ch", "ctx"),
        P(),
        P(),
        P("ch", None, None),
        P("ch", None, None),
        P("ch"),
        P("ch"),
        P("ch", "ctx"),
    )
    out_specs = (
        P("ch", "ctx"),
        P("ch", "ctx"),
        P(),
        P(),
        P("ch", None, None),
        P("ch", None, None),
        P("ch"),
        P("ch"),
    )
    return jax.shard_map(
        on_device, mesh=mesh, in_specs=in_specs, out_specs=out_specs, check_vma=False
    )
```

```python
import functools

import jax
import jax.numpy as jnp
from jax import lax
from jax.experimental import pallas as pl
from jax.experimental.pallas import tpu as pltpu
from jax.sharding import PartitionSpec as P

BF = jnp.bfloat16
F32 = jnp.float32
NB = 64
BLK = 512
CB = 8
CS = 160
KCH = 20
W = 256
HALF = 128


def dot(a, b, dims=((1,), (0,))):
    return lax.dot_general(a, b, (dims, ((), ())), preferred_element_type=F32)


NN = ((1,), (0,))
NT = ((1,), (1,))
TN = ((0,), (0,))


def iota(shape, axis):
    return lax.broadcasted_iota(jnp.int32, shape, axis)


def ones_where(cond):
    return jnp.where(cond, 1.0, 0.0).astype(BF)


def call(body, out_shapes, *args, scratch=(), smem=(), after=()):
    specs = [
        pl.BlockSpec(memory_space=pltpu.SMEM if at in smem else pltpu.VMEM)
        for at in range(len(args))
    ]
    specs += [pl.BlockSpec(memory_space=pl.ANY) for _ in after]
    used, held = len(args), len(args) + len(after)

    def run(*refs):
        body(*refs[:used], *refs[held:])

    return pl.pallas_call(
        run,
        out_shape=[jax.ShapeDtypeStruct(s, d) for s, d in out_shapes],
        in_specs=specs,
        out_specs=[pl.BlockSpec(memory_space=pltpu.VMEM) for _ in out_shapes],
        scratch_shapes=list(scratch),
        compiler_params=pltpu.CompilerParams(vmem_limit_bytes=48 * 1024 * 1024),
    )(*args, *after)


def group_of(rank, flag_ref):
    return ((flag_ref[1] - rank % 4) & 3) * 2 + ((rank // 4) ^ flag_ref[2])


def transpose_input(x_ref, xt_ref):
    zeros = jnp.zeros((W - CS, BLK), F32)
    xt = jnp.concatenate([x_ref[...].astype(F32), zeros], axis=0).T
    xt_ref[...] = xt.reshape(NB, 8, W).astype(BF)


def pack_cotangent(cot_ref, second_ref, out_ref, pad_ref):
    out_ref[0:CS, :] = cot_ref[...]
    pad_ref[...] = jnp.zeros(pad_ref.shape, F32)
    pad_ref[0:KCH, 0:64] = second_ref[...].astype(F32)
    more = jnp.concatenate([pltpu.roll(pad_ref[16:24, :], 64, 1), jnp.zeros((8, HALF), F32)], axis=0)
    tile = (pad_ref[0:16, :] + more).astype(BF)
    out_ref[CS:CS + 16, :] = jnp.concatenate([tile] * 4, axis=1)


def prepare(gain_ref, bias_ref, cross_ref, gain_out_ref, bias_out_ref, kron_ref, kront_ref, pad_ref):
    for row, out_ref in ((gain_ref, gain_out_ref), (bias_ref, bias_out_ref)):
        pad_ref[...] = jnp.zeros(pad_ref.shape, F32)
        pad_ref[:, 0:CS] = jnp.broadcast_to(row[...], (HALF, CS))
        out_ref[...] = pad_ref[...].T[:CS]
    spread = ones_where(iota((BLK, NB), 0) // 8 == iota((BLK, NB), 1))
    same = iota((BLK, BLK), 0) % 8 == iota((BLK, BLK), 1) % 8
    half = dot(spread, cross_ref[...], NN).astype(BF)
    kron_ref[...] = jnp.where(same, dot(half, spread, NT), 0.0).astype(BF)
    half = dot(spread, cross_ref[...], NT).astype(BF)
    kront_ref[...] = jnp.where(same, dot(half, spread, NT), 0.0).astype(BF)


def cross_forward(kront_ref, cols_ref, out_ref):
    cols = cols_ref[...].astype(F32).reshape(BLK, W).astype(BF)
    out_ref[...] = dot(kront_ref[...], cols).reshape(NB, 8, W).astype(BF)


def channel(u_ref, block_ref, x_ref, gain_ref, bias_ref, weight_ref, side_ref, other_ref,
            flag_ref, send_ref, act_ref, hidden_ref, rest_ref, factor_ref):
    cots = [ref.at[s] for ref in (side_ref, other_ref) for s in range(4)]
    q = flag_ref[0]
    u = u_ref[...].astype(F32).reshape(BLK, W).astype(BF)
    mixed = dot(u, block_ref[...], TN)[:CS].astype(BF).astype(F32)
    x = x_ref[...].astype(F32)
    gain = jnp.concatenate([gain_ref[...]] * 4, axis=1)
    bias = jnp.concatenate([bias_ref[...]] * 4, axis=1)
    gate = jax.nn.sigmoid(x * gain + bias)
    hidden = (x + gate * mixed).astype(BF)
    hidden_ref[...] = hidden
    weight = weight_ref[0]
    pre = dot(weight, hidden)
    root = 0.7978845608028654
    square = pre * pre
    curve = jnp.tanh(root * (pre + 0.044715 * (square * pre)))
    act = (pre * (0.5 * (1.0 + curve))).astype(BF)
    act_ref[...] = act
    act = act.astype(F32)
    slope = 0.5 * (1.0 + curve) + pre * (0.5 * (1.0 - curve * curve)) * (
        root * (1.0 + (3 * 0.044715) * square)
    )
    tiles = jnp.concatenate([cot[CS:CS + 16, 0:HALF].astype(F32) for cot in cots], axis=0).astype(BF)
    k, m = iota((CS, HALF), 0), iota((CS, HALF), 1)
    start = KCH * group_of(m // 16, flag_ref)
    low = dot(ones_where(k == start + m % 16), tiles)
    high = dot(ones_where((k == start + 16 + m % 16) & (m % 16 < 4)), tiles)
    second = jnp.where(m < 64, low + pltpu.roll(high, 64, 1), 0.0).astype(BF)
    pair, rank = iota((HALF, HALF), 0), iota((HALF, HALF), 1)
    group = group_of(rank, flag_ref)
    factor_ref[...] = dot(second, ones_where((pair == q * CB + group) & (rank < CB)))
    back = dot(second, ones_where((pair == group * CB + q) & (rank < CB)))
    d_act = jnp.zeros((CS, BLK), F32)
    grad_second = jnp.zeros((CS, HALF), F32)
    for r in range(CB):
        cot = cots[r][0:CS, :].astype(F32)
        d_act = d_act + back[:, r:r + 1] * cot
        column = jnp.sum(cot * act, axis=1, keepdims=True)
        grad_second = jnp.where(m == 32 + CB * group_of(r, flag_ref) + q, column, grad_second)
    d_pre = (d_act.astype(BF).astype(F32) * slope).astype(BF)
    zeros = jnp.zeros((W - CS, BLK), F32)
    tall = jnp.concatenate([hidden.astype(F32), zeros], axis=0).astype(BF)
    grad_first = dot(d_pre, tall, NT)
    d_hidden = side_ref[0, 0:CS, :].astype(F32) + dot(weight, d_pre, TN)
    d_mixed = jnp.concatenate([d_hidden * gate, zeros], axis=0).astype(BF)
    d_gate = d_hidden * mixed * gate * (1.0 - gate)
    grad_gain = jnp.sum(d_gate * x, axis=1, keepdims=True)
    grad_bias = jnp.sum(d_gate, axis=1, keepdims=True)
    rest_ref[...] = d_hidden + d_gate * gain
    v = dot(block_ref[...], d_mixed, NT)
    left, right = grad_first[:, :HALF], grad_first[:, HALF:]
    misc_b = jnp.where(m < 64, pltpu.roll(left, 32, 1), pltpu.roll(right, 64, 1))
    misc_b = jnp.where(m == 96, grad_gain, jnp.where(m == 97, grad_bias, misc_b))
    misc = jnp.concatenate([left, misc_b, grad_second, jnp.zeros((32, HALF), F32)], axis=0)
    right = jnp.where(iota((BLK, HALF), 1) < 32, v[:, HALF:], misc).reshape(NB, 8, HALF)
    left = v[:, :HALF].reshape(NB, 8, HALF)
    send_ref[:, 0:16, :] = jnp.concatenate([left, right], axis=1).astype(BF)
    d_block = dot(u, d_mixed, NN)
    parts = [d_block[:, HALF * s:HALF * (s + 1)].reshape(NB, 8, HALF) for s in range(4)]
    send_ref[:, 16:48, :] = jnp.concatenate(parts, axis=1).astype(BF)


def cross_backward(recv_ref, x_ref, kron_ref, part_ref, d_input_ref):
    head = recv_ref[:, 0:16, :].astype(F32)
    low = iota((NB, 8, HALF), 2) < 32
    left, right = head[:, 0:8, :], head[:, 8:16, :]
    v = jnp.concatenate(
        [left.reshape(BLK, HALF), jnp.where(low, right, 0.0).reshape(BLK, HALF)], axis=1
    ).astype(BF)
    part_ref[64:72, :] = jnp.sum(right, axis=0)
    d_input_ref[...] = dot(kron_ref[...], v).astype(BF)
    x = x_ref[...].astype(F32).reshape(BLK, W).astype(BF)
    pairs = dot(x, v, NT)
    same = iota((BLK, BLK), 0) % 8 == iota((BLK, BLK), 1) % 8
    rows = jnp.sum(jnp.where(same, pairs, 0.0).reshape(NB, 8, BLK), axis=1)
    high = rows.astype(BF)
    rest = (rows - high.astype(F32)).astype(BF)
    at, lane = iota((BLK, HALF), 0) // 8, iota((BLK, HALF), 1)
    cross = jnp.zeros((32, HALF), F32)
    for s in range(2):
        gather = ones_where(at == lane - 64 * s)
        cross = cross + dot(high[32 * s:32 * s + 32], gather) + dot(rest[32 * s:32 * s + 32], gather)
    part_ref[32:64, :] = cross
    part_ref[0:32, :] = jnp.sum(recv_ref[:, 16:48, :].astype(F32), axis=0)


def add_parts(a_ref, b_ref, out_ref):
    out_ref[...] = a_ref[...] + b_ref[...]


def pack_last(a_ref, b_ref, c_ref, d_ref, own_ref, d_input_ref, flag_ref, send_ref):
    even = a_ref[...] + c_ref[...]
    odd = b_ref[...] + d_ref[...]
    total = even + odd
    misc = jnp.where(flag_ref[3] > 0, total[64:72], own_ref[64:72, :])
    d_input = d_input_ref[...].astype(F32)
    left = d_input[:, :HALF].reshape(NB, 8, HALF)
    right = jnp.where(
        iota((NB, 8, HALF), 2) < 32, d_input[:, HALF:].reshape(NB, 8, HALF), misc[None]
    )
    send_ref[:, 0:16, :] = jnp.concatenate([left, right], axis=1).astype(BF)
    first = flag_ref[2] == 0
    block = jnp.where(first, total[0:16], total[16:32])
    cross = jnp.where(first, total[32:48], total[48:64])
    tail = jnp.concatenate([block, cross], axis=0).astype(BF)
    send_ref[:, 16:48, :] = jnp.broadcast_to(tail[None], (NB, 32, HALF))


def finish_output(hidden_ref, factor_ref, side_ref, other_ref, out_ref):
    acts = [ref.at[s] for ref in (side_ref, other_ref) for s in range(4)]
    factor = factor_ref[...]
    branch = jnp.zeros((CS, BLK), F32)
    for r in range(CB):
        branch = branch + factor[:, r:r + 1] * acts[r][...].astype(F32)
    out_ref[...] = (hidden_ref[...].astype(F32) + branch.astype(BF).astype(F32)).astype(BF)


def finish_input(recv_ref, rest_ref, flag_ref, grad_ref, first_ref, second_ref, gain_ref, bias_ref):
    head = recv_ref[:, 0:16, :].astype(F32)
    left, misc = head[:, 0:8, :], head[:, 8:16, :].reshape(BLK, HALF)
    low = iota((BLK, HALF), 1) < 32
    d_input = jnp.concatenate([left.reshape(BLK, HALF), jnp.where(low, misc, 0.0)], axis=1)
    grad_ref[...] = (rest_ref[...] + d_input.T[:CS]).astype(BF)
    a, b = misc[0:CS], misc[CS:2 * CS]
    first_ref[0, :, 0:HALF] = jnp.where(iota((CS, HALF), 1) >= 32, a, pltpu.roll(b, 96, 1))
    first_ref[0, :, HALF:CS] = pltpu.roll(b, 64, 1)[:, 0:32]
    rows = misc[CS:CS + W].T
    gain_ref[...] = rows[96:97, 0:CS]
    bias_ref[...] = rows[97:98, 0:CS]
    pick = ones_where(iota((KCH, CS), 1) == iota((KCH, CS), 0) + KCH * flag_ref[0])
    second = dot(pick, misc[2 * CS:3 * CS].astype(BF))
    second_ref[...] = pltpu.roll(second, 96, 1)[:, 0:64]


def finish_sums(recv_ref, swap_ref, flag_ref, block_ref, cross_ref):
    first = flag_ref[2] == 0
    recv, swap = recv_ref[:, 16:48, :].astype(F32), swap_ref[:, 16:48, :].astype(F32)
    low, high = jnp.where(first, recv, swap), jnp.where(first, swap, recv)
    for s, half in enumerate((low, high)):
        for t in range(2):
            at = HALF * (2 * s + t)
            block_ref[:, at:at + HALF] = half[:, 8 * t:8 * t + 8, :].reshape(BLK, HALF)
    cross = jnp.concatenate(
        [jnp.sum(low[:, 16:32, :], axis=0), jnp.sum(high[:, 16:32, :], axis=0)], axis=0
    )
    cross_ref[0:32, :] = cross[:, 0:64]
    cross_ref[32:64, :] = pltpu.roll(cross, 64, 1)[:, 0:64]


PAIR = [(i, i ^ 1) for i in range(CB)]


def shift(s):
    return [(i, (i + 2 * s) % CB) for i in range(CB)]


def along(x):
    return [lax.ppermute(x, "ch", shift(s)) for s in (1, 2, 3)]


def across(x, arrived):
    side = jnp.stack([x] + arrived)
    return side, lax.ppermute(side, "ch", PAIR)


def on_device(layer_input, w_block, w_cross, ch_first, ch_second, gate_gain, gate_bias, cotangent):
    swap = functools.partial(
        lax.all_to_all, axis_name="ctx", split_axis=0, concat_axis=0, tiled=True
    )
    ctx, ch = lax.axis_index("ctx"), lax.axis_index("ch")
    second_sum = (ctx >= 40) & (ctx < 60)
    flag = jnp.stack([ch, ch // 2, ch % 2, second_sum.astype(jnp.int32)]).astype(jnp.int32)
    (xt,) = call(transpose_input, [((NB, 8, W), BF)], layer_input)
    (packed,) = call(
        pack_cotangent, [((CS + 16, BLK), BF)], cotangent, ch_second.reshape(KCH, CB * CB),
        scratch=[pltpu.VMEM((24, HALF), F32)],
    )
    x_cols = swap(xt)
    arrived = along(packed)
    gain, bias, kron, kront = call(
        prepare,
        [((CS, HALF), F32), ((CS, HALF), F32), ((BLK, BLK), BF), ((BLK, BLK), BF)],
        gate_gain.reshape(1, CS), gate_bias.reshape(1, CS), w_cross,
        scratch=[pltpu.VMEM((HALF, W), F32)],
    )
    (u_cols,) = call(cross_forward, [((NB, 8, W), BF)], kront, x_cols, after=arrived)
    u = swap(u_cols)
    cots = across(packed, arrived)
    send, act, hidden, rest, factor = call(
        channel,
        [((NB, 48, HALF), BF), ((CS, BLK), BF), ((CS, BLK), BF), ((CS, BLK), F32), ((CS, HALF), F32)],
        u, w_block, layer_input, gain, bias, ch_first, *cots, flag,
        smem=(8,),
    )
    recv = swap(send)
    arrived = along(act)
    part, d_input = call(
        cross_backward, [((72, HALF), F32), ((BLK, W), BF)], recv, x_cols, kron, after=arrived
    )
    (total,) = call(add_parts, [((72, HALF), F32)], part, lax.ppermute(part, "ch", PAIR))
    (send,) = call(
        pack_last, [((NB, 48, HALF), BF)], total, *along(total), part, d_input, flag, smem=(6,)
    )
    recv = swap(send)
    acts = across(act, arrived)
    (output,) = call(finish_output, [((CS, BLK), BF)], hidden, factor, *acts)
    swapped = lax.ppermute(recv, "ch", PAIR)
    grad_input, grad_first, grad_second, grad_gain, grad_bias = call(
        finish_input,
        [((CS, BLK), BF), ((1, CS, CS), F32), ((KCH, CB * CB), F32), ((1, CS), F32), ((1, CS), F32)],
        recv, rest, flag,
        smem=(2,),
    )
    grad_block, grad_cross = call(
        finish_sums, [((BLK, BLK), F32), ((NB, NB), F32)], recv, swapped, flag, smem=(2,)
    )
    return (
        output,
        grad_input,
        grad_block,
        grad_cross,
        grad_first,
        grad_second.reshape(KCH, CB, CB),
        grad_gain.reshape(CS),
        grad_bias.reshape(CS),
    )


def solution(mesh):
    in_specs = (
        P("ch", "ctx"),
        P(),
        P(),
        P("ch", None, None),
        P("ch", None, None),
        P("ch"),
        P("ch"),
        P("ch", "ctx"),
    )
    out_specs = (
        P("ch", "ctx"),
        P("ch", "ctx"),
        P(),
        P(),
        P("ch", None, None),
        P("ch", None, None),
        P("ch"),
        P("ch"),
    )
    return jax.shard_map(
        on_device, mesh=mesh, in_specs=in_specs, out_specs=out_specs, check_vma=False
    )
```

```python
import functools

import jax
import jax.numpy as jnp
from jax import lax
from jax.experimental import pallas as pl
from jax.experimental.pallas import tpu as pltpu
from jax.sharding import PartitionSpec as P

BF = jnp.bfloat16
F32 = jnp.float32
NB = 64
BLK = 512
CB = 8
CS = 160
KCH = 20
W = 256
HALF = 128


def dot(a, b, dims=((1,), (0,))):
    return lax.dot_general(a, b, (dims, ((), ())), preferred_element_type=F32)


NN = ((1,), (0,))
NT = ((1,), (1,))
TN = ((0,), (0,))


def iota(shape, axis):
    return lax.broadcasted_iota(jnp.int32, shape, axis)


def ones_where(cond):
    return jnp.where(cond, 1.0, 0.0).astype(BF)


def call(body, out_shapes, *args, scratch=(), smem=(), after=()):
    specs = [
        pl.BlockSpec(memory_space=pltpu.SMEM if at in smem else pltpu.VMEM)
        for at in range(len(args))
    ]
    specs += [pl.BlockSpec(memory_space=pl.ANY) for _ in after]
    used, held = len(args), len(args) + len(after)

    def run(*refs):
        body(*refs[:used], *refs[held:])

    return pl.pallas_call(
        run,
        out_shape=[jax.ShapeDtypeStruct(s, d) for s, d in out_shapes],
        in_specs=specs,
        out_specs=[pl.BlockSpec(memory_space=pltpu.VMEM) for _ in out_shapes],
        scratch_shapes=list(scratch),
        compiler_params=pltpu.CompilerParams(vmem_limit_bytes=48 * 1024 * 1024),
    )(*args, *after)


def transpose_input(x_ref, xt_ref):
    zeros = jnp.zeros((W - CS, BLK), F32)
    xt = jnp.concatenate([x_ref[...].astype(F32), zeros], axis=0).T
    xt_ref[...] = xt.reshape(NB, 8, W).astype(BF)


def pack_cotangent(cot_ref, second_ref, out_ref, pad_ref):
    out_ref[0:CS, :] = cot_ref[...]
    pad_ref[...] = jnp.zeros(pad_ref.shape, F32)
    pad_ref[0:KCH, 0:64] = second_ref[...].astype(F32)
    more = jnp.concatenate([pltpu.roll(pad_ref[16:24, :], 64, 1), jnp.zeros((8, HALF), F32)], axis=0)
    tile = (pad_ref[0:16, :] + more).astype(BF)
    out_ref[CS:CS + 16, :] = jnp.concatenate([tile] * 4, axis=1)


def prepare(gain_ref, bias_ref, cross_ref, gain_out_ref, bias_out_ref, kron_ref, kront_ref, pad_ref):
    for row, out_ref in ((gain_ref, gain_out_ref), (bias_ref, bias_out_ref)):
        pad_ref[...] = jnp.zeros(pad_ref.shape, F32)
        pad_ref[:, 0:CS] = jnp.broadcast_to(row[...], (HALF, CS))
        out_ref[...] = pad_ref[...].T[:CS]
    spread = ones_where(iota((BLK, NB), 0) // 8 == iota((BLK, NB), 1))
    same = iota((BLK, BLK), 0) % 8 == iota((BLK, BLK), 1) % 8
    half = dot(spread, cross_ref[...], NN).astype(BF)
    kron_ref[...] = jnp.where(same, dot(half, spread, NT), 0.0).astype(BF)
    half = dot(spread, cross_ref[...], NT).astype(BF)
    kront_ref[...] = jnp.where(same, dot(half, spread, NT), 0.0).astype(BF)


def cross_forward(kront_ref, cols_ref, out_ref):
    cols = cols_ref[...].astype(F32).reshape(BLK, W).astype(BF)
    out_ref[...] = dot(kront_ref[...], cols).reshape(NB, 8, W).astype(BF)


def channel(u_ref, block_ref, x_ref, gain_ref, bias_ref, weight_ref, cot_ref,
            cots_ref, flag_ref, send_ref, act_ref, hidden_ref, rest_ref, factor_ref):
    cots = [cots_ref.at[g] for g in range(CB)]
    q = flag_ref[0]
    u = u_ref[...].astype(F32).reshape(BLK, W).astype(BF)
    mixed = dot(u, block_ref[...], TN)[:CS].astype(BF).astype(F32)
    x = x_ref[...].astype(F32)
    gain = jnp.concatenate([gain_ref[...]] * 4, axis=1)
    bias = jnp.concatenate([bias_ref[...]] * 4, axis=1)
    gate = jax.nn.sigmoid(x * gain + bias)
    hidden = (x + gate * mixed).astype(BF)
    hidden_ref[...] = hidden
    weight = weight_ref[0]
    pre = dot(weight, hidden)
    root = 0.7978845608028654
    square = pre * pre
    curve = jnp.tanh(root * (pre + 0.044715 * (square * pre)))
    act = (pre * (0.5 * (1.0 + curve))).astype(BF)
    act_ref[...] = act
    act = act.astype(F32)
    slope = 0.5 * (1.0 + curve) + pre * (0.5 * (1.0 - curve * curve)) * (
        root * (1.0 + (3 * 0.044715) * square)
    )
    tiles = jnp.concatenate([cot[CS:CS + 16, 0:HALF].astype(F32) for cot in cots], axis=0).astype(BF)
    k, m = iota((CS, HALF), 0), iota((CS, HALF), 1)
    start = KCH * (m // 16)
    low = dot(ones_where(k == start + m % 16), tiles)
    high = dot(ones_where((k == start + 16 + m % 16) & (m % 16 < 4)), tiles)
    second = jnp.where(m < 64, low + pltpu.roll(high, 64, 1), 0.0).astype(BF)
    pair, group = iota((HALF, HALF), 0), iota((HALF, HALF), 1)
    factor_ref[...] = dot(second, ones_where((pair == q * CB + group) & (group < CB)))
    back = dot(second, ones_where((pair == group * CB + q) & (group < CB)))
    d_act = jnp.zeros((CS, BLK), F32)
    grad_second = jnp.zeros((CS, HALF), F32)
    for g in range(CB):
        cot = cots[g][0:CS, :].astype(F32)
        d_act = d_act + back[:, g:g + 1] * cot
        column = jnp.sum(cot * act, axis=1, keepdims=True)
        grad_second = jnp.where(m == 32 + CB * g + q, column, grad_second)
    d_pre = (d_act.astype(BF).astype(F32) * slope).astype(BF)
    zeros = jnp.zeros((W - CS, BLK), F32)
    tall = jnp.concatenate([hidden.astype(F32), zeros], axis=0).astype(BF)
    grad_first = dot(d_pre, tall, NT)
    d_hidden = cot_ref[...].astype(F32) + dot(weight, d_pre, TN)
    d_mixed = jnp.concatenate([d_hidden * gate, zeros], axis=0).astype(BF)
    d_gate = d_hidden * mixed * gate * (1.0 - gate)
    grad_gain = jnp.sum(d_gate * x, axis=1, keepdims=True)
    grad_bias = jnp.sum(d_gate, axis=1, keepdims=True)
    rest_ref[...] = d_hidden + d_gate * gain
    v = dot(block_ref[...], d_mixed, NT)
    left, right = grad_first[:, :HALF], grad_first[:, HALF:]
    misc_b = jnp.where(m < 64, pltpu.roll(left, 32, 1), pltpu.roll(right, 64, 1))
    misc_b = jnp.where(m == 96, grad_gain, jnp.where(m == 97, grad_bias, misc_b))
    misc = jnp.concatenate([left, misc_b, grad_second, jnp.zeros((32, HALF), F32)], axis=0)
    right = jnp.where(iota((BLK, HALF), 1) < 32, v[:, HALF:], misc).reshape(NB, 8, HALF)
    left = v[:, :HALF].reshape(NB, 8, HALF)
    send_ref[:, 0:16, :] = jnp.concatenate([left, right], axis=1).astype(BF)
    d_block = dot(u, d_mixed, NN)
    parts = [d_block[:, HALF * s:HALF * (s + 1)].reshape(NB, 8, HALF) for s in range(4)]
    send_ref[:, 16:48, :] = jnp.concatenate(parts, axis=1).astype(BF)


def cross_backward(recv_ref, x_ref, kron_ref, send_ref, d_input_ref, misc_ref):
    head = recv_ref[:, 0:16, :].astype(F32)
    low = iota((NB, 8, HALF), 2) < 32
    left, right = head[:, 0:8, :], head[:, 8:16, :]
    v = jnp.concatenate(
        [left.reshape(BLK, HALF), jnp.where(low, right, 0.0).reshape(BLK, HALF)], axis=1
    ).astype(BF)
    misc = jnp.sum(right, axis=0)
    misc_ref[...] = misc
    d_input_ref[...] = dot(kron_ref[...], v).astype(BF)
    x = x_ref[...].astype(F32).reshape(BLK, W).astype(BF)
    pairs = dot(x, v, NT)
    same = iota((BLK, BLK), 0) % 8 == iota((BLK, BLK), 1) % 8
    rows = jnp.sum(jnp.where(same, pairs, 0.0).reshape(NB, 8, BLK), axis=1)
    high = rows.astype(BF)
    rest = (rows - high.astype(F32)).astype(BF)
    at, lane = iota((BLK, HALF), 0) // 8, iota((BLK, HALF), 1)
    cross = jnp.zeros((32, HALF), F32)
    for s in range(2):
        gather = ones_where(at == lane - 64 * s)
        cross = cross + dot(high[32 * s:32 * s + 32], gather) + dot(rest[32 * s:32 * s + 32], gather)
    tail = jnp.sum(recv_ref[:, 16:48, :].astype(F32), axis=0)
    send_ref[...] = jnp.concatenate([tail, cross, misc], axis=0)


def pack_last(recv_ref, own_ref, d_input_ref, flag_ref, send_ref):
    total = jnp.sum(recv_ref[...], axis=0)
    misc = jnp.where(flag_ref[3] > 0, total[64:72], own_ref[...])
    d_input = d_input_ref[...].astype(F32)
    left = d_input[:, :HALF].reshape(NB, 8, HALF)
    right = jnp.where(
        iota((NB, 8, HALF), 2) < 32, d_input[:, HALF:].reshape(NB, 8, HALF), misc[None]
    )
    send_ref[:, 0:16, :] = jnp.concatenate([left, right], axis=1).astype(BF)
    first = flag_ref[2] == 0
    block = jnp.where(first, total[0:16], total[16:32])
    cross = jnp.where(first, total[32:48], total[48:64])
    tail = jnp.concatenate([block, cross], axis=0).astype(BF)
    send_ref[:, 16:48, :] = jnp.broadcast_to(tail[None], (NB, 32, HALF))


def split_last(recv_ref, out_ref):
    recv = recv_ref[:, 16:32, :].astype(F32)
    left = recv[:, 0:8, :].reshape(BLK, HALF)
    right = recv[:, 8:16, :].reshape(BLK, HALF)
    out_ref[0:BLK, :] = jnp.concatenate([left, right], axis=1).astype(BF)
    cross = jnp.sum(recv_ref[:, 32:48, :].astype(F32), axis=0)
    out_ref[BLK:BLK + 16, :] = jnp.concatenate([cross, cross], axis=1).astype(BF)


def finish_output(hidden_ref, factor_ref, acts_ref, out_ref):
    factor = factor_ref[...]
    branch = jnp.zeros((CS, BLK), F32)
    for g in range(CB):
        branch = branch + factor[:, g:g + 1] * acts_ref[g].astype(F32)
    out_ref[...] = (hidden_ref[...].astype(F32) + branch.astype(BF).astype(F32)).astype(BF)


def finish_input(recv_ref, rest_ref, flag_ref, grad_ref, first_ref, second_ref, gain_ref, bias_ref):
    head = recv_ref[:, 0:16, :].astype(F32)
    left, misc = head[:, 0:8, :], head[:, 8:16, :].reshape(BLK, HALF)
    low = iota((BLK, HALF), 1) < 32
    d_input = jnp.concatenate([left.reshape(BLK, HALF), jnp.where(low, misc, 0.0)], axis=1)
    grad_ref[...] = (rest_ref[...] + d_input.T[:CS]).astype(BF)
    a, b = misc[0:CS], misc[CS:2 * CS]
    first_ref[0, :, 0:HALF] = jnp.where(iota((CS, HALF), 1) >= 32, a, pltpu.roll(b, 96, 1))
    first_ref[0, :, HALF:CS] = pltpu.roll(b, 64, 1)[:, 0:32]
    rows = misc[CS:CS + W].T
    gain_ref[...] = rows[96:97, 0:CS]
    bias_ref[...] = rows[97:98, 0:CS]
    pick = ones_where(iota((KCH, CS), 1) == iota((KCH, CS), 0) + KCH * flag_ref[0])
    second = dot(pick, misc[2 * CS:3 * CS].astype(BF))
    second_ref[...] = pltpu.roll(second, 96, 1)[:, 0:64]


def finish_sums(own_ref, swap_ref, flag_ref, block_ref, cross_ref):
    first = flag_ref[2] == 0
    own, swap = own_ref[...].astype(F32), swap_ref[...].astype(F32)
    low, high = jnp.where(first, own, swap), jnp.where(first, swap, own)
    block_ref[:, 0:W] = low[0:BLK]
    block_ref[:, W:BLK] = high[0:BLK]
    cross = jnp.concatenate([low[BLK:, 0:HALF], high[BLK:, 0:HALF]], axis=0)
    cross_ref[0:32, :] = cross[:, 0:64]
    cross_ref[32:64, :] = pltpu.roll(cross, 64, 1)[:, 0:64]


PAIR = [(i, i ^ 1) for i in range(CB)]


def on_device(layer_input, w_block, w_cross, ch_first, ch_second, gate_gain, gate_bias, cotangent):
    swap = functools.partial(lax.all_to_all, split_axis=0, concat_axis=0, tiled=True)
    ctx, ch = lax.axis_index("ctx"), lax.axis_index("ch")
    second_sum = (ctx >= 40) & (ctx < 60)
    flag = jnp.stack([ch, ch // 2, ch % 2, second_sum.astype(jnp.int32)]).astype(jnp.int32)
    (xt,) = call(transpose_input, [((NB, 8, W), BF)], layer_input)
    (packed,) = call(
        pack_cotangent, [((CS + 16, BLK), BF)], cotangent, ch_second.reshape(KCH, CB * CB),
        scratch=[pltpu.VMEM((24, HALF), F32)],
    )
    x_cols = swap(xt, "ctx")
    cots = lax.all_gather(packed, "ch")
    gain, bias, kron, kront = call(
        prepare,
        [((CS, HALF), F32), ((CS, HALF), F32), ((BLK, BLK), BF), ((BLK, BLK), BF)],
        gate_gain.reshape(1, CS), gate_bias.reshape(1, CS), w_cross,
        scratch=[pltpu.VMEM((HALF, W), F32)],
    )
    (u_cols,) = call(cross_forward, [((NB, 8, W), BF)], kront, x_cols)
    u = swap(u_cols, "ctx")
    send, act, hidden, rest, factor = call(
        channel,
        [((NB, 48, HALF), BF), ((CS, BLK), BF), ((CS, BLK), BF), ((CS, BLK), F32), ((CS, HALF), F32)],
        u, w_block, layer_input, gain, bias, ch_first, cotangent, cots, flag,
        smem=(8,),
    )
    recv = swap(send, "ctx")
    acts = lax.all_gather(act, "ch")
    send, d_input, misc = call(
        cross_backward, [((72, HALF), F32), ((BLK, W), BF), ((8, HALF), F32)], recv, x_cols, kron,
    )
    (send,) = call(
        pack_last, [((NB, 48, HALF), BF)], lax.all_gather(send, "ch"), misc, d_input, flag, smem=(3,)
    )
    recv = swap(send, "ctx")
    (output,) = call(finish_output, [((CS, BLK), BF)], hidden, factor, acts)
    (half,) = call(split_last, [((BLK + 16, W), BF)], recv, after=[output])
    swapped = lax.ppermute(half, "ch", PAIR)
    grad_input, grad_first, grad_second, grad_gain, grad_bias = call(
        finish_input,
        [((CS, BLK), BF), ((1, CS, CS), F32), ((KCH, CB * CB), F32), ((1, CS), F32), ((1, CS), F32)],
        recv, rest, flag,
        smem=(2,),
    )
    grad_block, grad_cross = call(
        finish_sums, [((BLK, BLK), F32), ((NB, NB), F32)], half, swapped, flag, smem=(2,)
    )
    return (
        output,
        grad_input,
        grad_block,
        grad_cross,
        grad_first,
        grad_second.reshape(KCH, CB, CB),
        grad_gain.reshape(CS),
        grad_bias.reshape(CS),
    )


def solution(mesh):
    in_specs = (
        P("ch", "ctx"),
        P(),
        P(),
        P("ch", None, None),
        P("ch", None, None),
        P("ch"),
        P("ch"),
        P("ch", "ctx"),
    )
    out_specs = (
        P("ch", "ctx"),
        P("ch", "ctx"),
        P(),
        P(),
        P("ch", None, None),
        P("ch", None, None),
        P("ch"),
        P("ch"),
    )
    return jax.shard_map(
        on_device, mesh=mesh, in_specs=in_specs, out_specs=out_specs, check_vma=False
    )
```

```python
import functools

import jax
import jax.numpy as jnp
from jax import lax
from jax.experimental import pallas as pl
from jax.experimental.pallas import tpu as pltpu
from jax.sharding import PartitionSpec as P

BF = jnp.bfloat16
F32 = jnp.float32
NB = 64
BLK = 512
CB = 8
CS = 160
KCH = 20
W = 256
HALF = 128


def dot(a, b, dims=((1,), (0,))):
    return lax.dot_general(a, b, (dims, ((), ())), preferred_element_type=F32)


NN = ((1,), (0,))
NT = ((1,), (1,))
TN = ((0,), (0,))


def iota(shape, axis):
    return lax.broadcasted_iota(jnp.int32, shape, axis)


def ones_where(cond):
    return jnp.where(cond, 1.0, 0.0).astype(BF)


def call(body, out_shapes, *args, scratch=(), smem=(), far=(), vmem=48, after=()):
    specs = [
        pl.BlockSpec(
            memory_space=pltpu.SMEM if at in smem else pl.ANY if at in far else pltpu.VMEM
        )
        for at in range(len(args))
    ]
    specs += [pl.BlockSpec(memory_space=pl.ANY) for _ in after]
    used, held = len(args), len(args) + len(after)

    def run(*refs):
        body(*refs[:used], *refs[held:])

    return pl.pallas_call(
        run,
        out_shape=[jax.ShapeDtypeStruct(s, d) for s, d in out_shapes],
        in_specs=specs,
        out_specs=[pl.BlockSpec(memory_space=pltpu.VMEM) for _ in out_shapes],
        scratch_shapes=list(scratch),
        compiler_params=pltpu.CompilerParams(vmem_limit_bytes=vmem * 1024 * 1024),
    )(*args, *after)


def begin(x_ref, cot_ref, second_ref, xt_ref, out_ref, x_in, cot_in, pad_ref, sems):
    x_copy = pltpu.make_async_copy(x_ref, x_in, sems.at[0])
    cot_copy = pltpu.make_async_copy(cot_ref, cot_in, sems.at[1])
    x_copy.start()
    cot_copy.start()
    pad_ref[...] = jnp.zeros(pad_ref.shape, F32)
    eye = ones_where(iota((KCH, KCH), 0) == iota((KCH, KCH), 1))
    pad_ref[0:KCH, 0:64] = dot(eye, second_ref[...], NT)
    more = jnp.concatenate([pltpu.roll(pad_ref[16:24, :], 64, 1), jnp.zeros((8, HALF), F32)], axis=0)
    tile = (pad_ref[0:16, :] + more).astype(BF)
    out_ref[CS:CS + 16, :] = jnp.concatenate([tile] * 4, axis=1)
    x_copy.wait()
    zeros = jnp.zeros((W - CS, BLK), F32)
    xt = jnp.concatenate([x_in[...].astype(F32), zeros], axis=0).T
    xt_ref[...] = xt.reshape(NB, 8, W).astype(BF)
    cot_copy.wait()
    out_ref[0:CS, :] = cot_in[...]


def prepare(gain_ref, bias_ref, cross_ref, gain_out_ref, bias_out_ref, kron_ref, kront_ref, pad_ref):
    for row, out_ref in ((gain_ref, gain_out_ref), (bias_ref, bias_out_ref)):
        pad_ref[...] = jnp.zeros(pad_ref.shape, F32)
        pad_ref[:, 0:CS] = jnp.broadcast_to(row[...], (HALF, CS))
        out_ref[...] = pad_ref[...].T[:CS]
    spread = ones_where(iota((BLK, NB), 0) // 8 == iota((BLK, NB), 1))
    same = iota((BLK, BLK), 0) % 8 == iota((BLK, BLK), 1) % 8
    half = dot(spread, cross_ref[...], NN).astype(BF)
    kron_ref[...] = jnp.where(same, dot(half, spread, NT), 0.0).astype(BF)
    half = dot(spread, cross_ref[...], NT).astype(BF)
    kront_ref[...] = jnp.where(same, dot(half, spread, NT), 0.0).astype(BF)


def cross_forward(kront_ref, cols_ref, out_ref):
    cols = cols_ref[...].astype(F32).reshape(BLK, W).astype(BF)
    out_ref[...] = dot(kront_ref[...], cols).reshape(NB, 8, W).astype(BF)


def channel(u_ref, block_ref, x_ref, gain_ref, bias_ref, weight_ref, cot_ref,
            far_ref, flag_ref, send_ref, act_ref, hidden_ref, rest_ref, factor_ref, cots_ref, sem):
    copy = pltpu.make_async_copy(far_ref, cots_ref, sem)
    copy.start()
    cots = [cots_ref.at[g] for g in range(CB)]
    q = flag_ref[0]
    u = u_ref[...].astype(F32).reshape(BLK, W).astype(BF)
    mixed = dot(u, block_ref[...], TN)[:CS].astype(BF).astype(F32)
    x = x_ref[...].astype(F32)
    gain = jnp.concatenate([gain_ref[...]] * 4, axis=1)
    bias = jnp.concatenate([bias_ref[...]] * 4, axis=1)
    gate = jax.nn.sigmoid(x * gain + bias)
    hidden = (x + gate * mixed).astype(BF)
    hidden_ref[...] = hidden
    weight = weight_ref[0]
    pre = dot(weight, hidden)
    root = 0.7978845608028654
    square = pre * pre
    curve = jnp.tanh(root * (pre + 0.044715 * (square * pre)))
    act = (pre * (0.5 * (1.0 + curve))).astype(BF)
    act_ref[...] = act
    act = act.astype(F32)
    slope = 0.5 * (1.0 + curve) + pre * (0.5 * (1.0 - curve * curve)) * (
        root * (1.0 + (3 * 0.044715) * square)
    )
    copy.wait()
    tiles = jnp.concatenate([cot[CS:CS + 16, 0:HALF].astype(F32) for cot in cots], axis=0).astype(BF)
    k, m = iota((CS, HALF), 0), iota((CS, HALF), 1)
    start = KCH * (m // 16)
    low = dot(ones_where(k == start + m % 16), tiles)
    high = dot(ones_where((k == start + 16 + m % 16) & (m % 16 < 4)), tiles)
    second = jnp.where(m < 64, low + pltpu.roll(high, 64, 1), 0.0).astype(BF)
    pair, group = iota((HALF, HALF), 0), iota((HALF, HALF), 1)
    factor_ref[...] = dot(second, ones_where((pair == q * CB + group) & (group < CB)))
    back = dot(second, ones_where((pair == group * CB + q) & (group < CB)))
    d_act = jnp.zeros((CS, BLK), F32)
    grad_second = jnp.zeros((CS, HALF), F32)
    for g in range(CB):
        cot = cots[g][0:CS, :].astype(F32)
        d_act = d_act + back[:, g:g + 1] * cot
        column = jnp.sum(cot * act, axis=1, keepdims=True)
        grad_second = jnp.where(m == 32 + CB * g + q, column, grad_second)
    d_pre = (d_act.astype(BF).astype(F32) * slope).astype(BF)
    zeros = jnp.zeros((W - CS, BLK), F32)
    tall = jnp.concatenate([hidden.astype(F32), zeros], axis=0).astype(BF)
    grad_first = dot(d_pre, tall, NT)
    d_hidden = cot_ref[...].astype(F32) + dot(weight, d_pre, TN)
    d_mixed = jnp.concatenate([d_hidden * gate, zeros], axis=0).astype(BF)
    d_gate = d_hidden * mixed * gate * (1.0 - gate)
    grad_gain = jnp.sum(d_gate * x, axis=1, keepdims=True)
    grad_bias = jnp.sum(d_gate, axis=1, keepdims=True)
    rest_ref[...] = d_hidden + d_gate * gain
    v = dot(block_ref[...], d_mixed, NT)
    left, right = grad_first[:, :HALF], grad_first[:, HALF:]
    misc_b = jnp.where(m < 64, pltpu.roll(left, 32, 1), pltpu.roll(right, 64, 1))
    misc_b = jnp.where(m == 96, grad_gain, jnp.where(m == 97, grad_bias, misc_b))
    misc = jnp.concatenate([left, misc_b, grad_second, jnp.zeros((32, HALF), F32)], axis=0)
    right = jnp.where(iota((BLK, HALF), 1) < 32, v[:, HALF:], misc).reshape(NB, 8, HALF)
    left = v[:, :HALF].reshape(NB, 8, HALF)
    send_ref[:, 0:16, :] = jnp.concatenate([left, right], axis=1).astype(BF)
    d_block = dot(u, d_mixed, NN)
    parts = [d_block[:, HALF * s:HALF * (s + 1)].reshape(NB, 8, HALF) for s in range(4)]
    send_ref[:, 16:48, :] = jnp.concatenate(parts, axis=1).astype(BF)


def cross_backward(recv_ref, x_ref, kron_ref, act_ref, send_ref, d_input_ref, misc_ref, pass_ref):
    pass_ref[...] = act_ref[...]
    head = recv_ref[:, 0:16, :].astype(F32)
    low = iota((NB, 8, HALF), 2) < 32
    left, right = head[:, 0:8, :], head[:, 8:16, :]
    v = jnp.concatenate(
        [left.reshape(BLK, HALF), jnp.where(low, right, 0.0).reshape(BLK, HALF)], axis=1
    ).astype(BF)
    misc = jnp.sum(right, axis=0)
    misc_ref[...] = misc
    d_input_ref[...] = dot(kron_ref[...], v).astype(BF)
    x = x_ref[...].astype(F32).reshape(BLK, W).astype(BF)
    pairs = dot(x, v, NT)
    same = iota((BLK, BLK), 0) % 8 == iota((BLK, BLK), 1) % 8
    rows = jnp.sum(jnp.where(same, pairs, 0.0).reshape(NB, 8, BLK), axis=1)
    high = rows.astype(BF)
    rest = (rows - high.astype(F32)).astype(BF)
    at, lane = iota((BLK, HALF), 0) // 8, iota((BLK, HALF), 1)
    cross = jnp.zeros((32, HALF), F32)
    for s in range(2):
        gather = ones_where(at == lane - 64 * s)
        cross = cross + dot(high[32 * s:32 * s + 32], gather) + dot(rest[32 * s:32 * s + 32], gather)
    tail = jnp.sum(recv_ref[:, 16:48, :].astype(F32), axis=0)
    send_ref[...] = jnp.concatenate([tail, cross, misc], axis=0)


def pack_last(recv_ref, own_ref, d_input_ref, flag_ref, send_ref):
    total = jnp.sum(recv_ref[...], axis=0)
    misc = jnp.where(flag_ref[3] > 0, total[64:72], own_ref[...])
    d_input = d_input_ref[...].astype(F32)
    left = d_input[:, :HALF].reshape(NB, 8, HALF)
    right = jnp.where(
        iota((NB, 8, HALF), 2) < 32, d_input[:, HALF:].reshape(NB, 8, HALF), misc[None]
    )
    send_ref[:, 0:16, :] = jnp.concatenate([left, right], axis=1).astype(BF)
    first = flag_ref[2] == 0
    block = jnp.where(first, total[0:16], total[16:32])
    cross = jnp.where(first, total[32:48], total[48:64])
    tail = jnp.concatenate([block, cross], axis=0).astype(BF)
    send_ref[:, 16:48, :] = jnp.broadcast_to(tail[None], (NB, 32, HALF))


def split_last(recv_ref, out_ref):
    recv = recv_ref[:, 16:32, :].astype(F32)
    left = recv[:, 0:8, :].reshape(BLK, HALF)
    right = recv[:, 8:16, :].reshape(BLK, HALF)
    out_ref[0:BLK, :] = jnp.concatenate([left, right], axis=1).astype(BF)
    cross = jnp.sum(recv_ref[:, 32:48, :].astype(F32), axis=0)
    out_ref[BLK:BLK + 16, :] = jnp.concatenate([cross, cross], axis=1).astype(BF)


def finish_input(recv_ref, rest_ref, hidden_ref, factor_ref, far_ref, flag_ref,
                 grad_ref, first_ref, second_ref, gain_ref, bias_ref, out_ref, acts_ref, sem):
    copy = pltpu.make_async_copy(far_ref, acts_ref, sem)
    copy.start()
    head = recv_ref[:, 0:16, :].astype(F32)
    left, misc = head[:, 0:8, :], head[:, 8:16, :].reshape(BLK, HALF)
    low = iota((BLK, HALF), 1) < 32
    d_input = jnp.concatenate([left.reshape(BLK, HALF), jnp.where(low, misc, 0.0)], axis=1)
    grad_ref[...] = (rest_ref[...] + d_input.T[:CS]).astype(BF)
    a, b = misc[0:CS], misc[CS:2 * CS]
    first_ref[0, :, 0:HALF] = jnp.where(iota((CS, HALF), 1) >= 32, a, pltpu.roll(b, 96, 1))
    first_ref[0, :, HALF:CS] = pltpu.roll(b, 64, 1)[:, 0:32]
    rows = misc[CS:CS + W].T
    gain_ref[...] = rows[96:97, 0:CS]
    bias_ref[...] = rows[97:98, 0:CS]
    pick = ones_where(iota((CS, KCH), 0) == iota((CS, KCH), 1) + KCH * flag_ref[0])
    second_ref[...] = dot(misc[2 * CS:3 * CS].astype(BF), pick, TN)[32:96]
    copy.wait()
    factor = factor_ref[...]
    branch = jnp.zeros((CS, BLK), F32)
    for g in range(CB):
        branch = branch + factor[:, g:g + 1] * acts_ref[g].astype(F32)
    out_ref[...] = (hidden_ref[...].astype(F32) + branch.astype(BF).astype(F32)).astype(BF)


def finish_sums(own_ref, swap_ref, flag_ref, block_ref, cross_ref):
    first = flag_ref[2] == 0
    own, swap = own_ref[...].astype(F32), swap_ref[...].astype(F32)
    low, high = jnp.where(first, own, swap), jnp.where(first, swap, own)
    block_ref[:, 0:W] = low[0:BLK]
    block_ref[:, W:BLK] = high[0:BLK]
    cross = jnp.concatenate([low[BLK:, 0:HALF], high[BLK:, 0:HALF]], axis=0)
    cross_ref[0:32, :] = cross[:, 0:64]
    cross_ref[32:64, :] = pltpu.roll(cross, 64, 1)[:, 0:64]


PAIR = [(i, i ^ 1) for i in range(CB)]


def on_device(layer_input, w_block, w_cross, ch_first, ch_second, gate_gain, gate_bias, cotangent):
    swap = functools.partial(lax.all_to_all, split_axis=0, concat_axis=0, tiled=True)
    ctx, ch = lax.axis_index("ctx"), lax.axis_index("ch")
    second_sum = (ctx >= 40) & (ctx < 60)
    flag = jnp.stack([ch, ch // 2, ch % 2, second_sum.astype(jnp.int32)]).astype(jnp.int32)
    xt, packed = call(
        begin, [((NB, 8, W), BF), ((CS + 16, BLK), BF)],
        layer_input, cotangent, ch_second.transpose(1, 2, 0).reshape(CB * CB, KCH),
        scratch=[pltpu.VMEM((CS, BLK), BF), pltpu.VMEM((CS, BLK), BF), pltpu.VMEM((24, HALF), F32),
                 pltpu.SemaphoreType.DMA((2,))],
        far=(0, 1), vmem=60,
    )
    x_cols = swap(xt, "ctx")
    cots = lax.all_gather(packed, "ch")
    gain, bias, kron, kront = call(
        prepare,
        [((CS, HALF), F32), ((CS, HALF), F32), ((BLK, BLK), BF), ((BLK, BLK), BF)],
        gate_gain.reshape(1, CS), gate_bias.reshape(1, CS), w_cross,
        scratch=[pltpu.VMEM((HALF, W), F32)],
    )
    (u_cols,) = call(cross_forward, [((NB, 8, W), BF)], kront, x_cols)
    u = swap(u_cols, "ctx")
    send, act, hidden, rest, factor = call(
        channel,
        [((NB, 48, HALF), BF), ((CS, BLK), BF), ((CS, BLK), BF), ((CS, BLK), F32), ((CS, HALF), F32)],
        u, w_block, layer_input, gain, bias, ch_first, cotangent, cots, flag,
        scratch=[pltpu.VMEM((CB, CS + 16, BLK), BF), pltpu.SemaphoreType.DMA], smem=(8,), far=(7,),
        vmem=60,
    )
    recv = swap(send, "ctx")
    send, d_input, misc, act = call(
        cross_backward,
        [((72, HALF), F32), ((BLK, W), BF), ((8, HALF), F32), ((CS, BLK), BF)],
        recv, x_cols, kron, act,
    )
    acts = lax.all_gather(act, "ch")
    (send,) = call(
        pack_last, [((NB, 48, HALF), BF)], lax.all_gather(send, "ch"), misc, d_input, flag, smem=(3,)
    )
    recv = swap(send, "ctx")
    (half,) = call(split_last, [((BLK + 16, W), BF)], recv)
    swapped = lax.ppermute(half, "ch", PAIR)
    grad_input, grad_first, grad_second, grad_gain, grad_bias, output = call(
        finish_input,
        [((CS, BLK), BF), ((1, CS, CS), F32), ((CB * CB, KCH), F32), ((1, CS), F32), ((1, CS), F32),
         ((CS, BLK), BF)],
        recv, rest, hidden, factor, acts, flag,
        scratch=[pltpu.VMEM((CB, CS, BLK), BF), pltpu.SemaphoreType.DMA], smem=(5,), far=(4,),
        vmem=60, after=[half],
    )
    grad_block, grad_cross = call(
        finish_sums, [((BLK, BLK), F32), ((NB, NB), F32)], half, swapped, flag, smem=(2,)
    )
    return (
        output,
        grad_input,
        grad_block,
        grad_cross,
        grad_first,
        grad_second.reshape(CB, CB, KCH).transpose(2, 0, 1),
        grad_gain.reshape(CS),
        grad_bias.reshape(CS),
    )


def solution(mesh):
    in_specs = (
        P("ch", "ctx"),
        P(),
        P(),
        P("ch", None, None),
        P("ch", None, None),
        P("ch"),
        P("ch"),
        P("ch", "ctx"),
    )
    out_specs = (
        P("ch", "ctx"),
        P("ch", "ctx"),
        P(),
        P(),
        P("ch", None, None),
        P("ch", None, None),
        P("ch"),
        P("ch"),
    )
    return jax.shard_map(
        on_device, mesh=mesh, in_specs=in_specs, out_specs=out_specs, check_vma=False
    )
```

```python
import functools

import jax
import jax.numpy as jnp
from jax import lax
from jax.experimental import pallas as pl
from jax.experimental.pallas import tpu as pltpu
from jax.sharding import PartitionSpec as P

BF = jnp.bfloat16
F32 = jnp.float32
NB = 64
BLK = 512
CB = 8
CS = 160
KCH = 20
W = 256
HALF = 128


def dot(a, b, dims=((1,), (0,))):
    return lax.dot_general(a, b, (dims, ((), ())), preferred_element_type=F32)


NN = ((1,), (0,))
NT = ((1,), (1,))
TN = ((0,), (0,))


def iota(shape, axis):
    return lax.broadcasted_iota(jnp.int32, shape, axis)


def ones_where(cond):
    return jnp.where(cond, 1.0, 0.0).astype(BF)


def call(body, out_shapes, *args, scratch=(), smem=(), far=(), vmem=48, after=()):
    specs = [
        pl.BlockSpec(
            memory_space=pltpu.SMEM if at in smem else pl.ANY if at in far else pltpu.VMEM
        )
        for at in range(len(args))
    ]
    specs += [pl.BlockSpec(memory_space=pl.ANY) for _ in after]
    used, held = len(args), len(args) + len(after)

    def run(*refs):
        body(*refs[:used], *refs[held:])

    return pl.pallas_call(
        run,
        out_shape=[jax.ShapeDtypeStruct(s, d) for s, d in out_shapes],
        in_specs=specs,
        out_specs=[pl.BlockSpec(memory_space=pltpu.VMEM) for _ in out_shapes],
        scratch_shapes=list(scratch),
        compiler_params=pltpu.CompilerParams(vmem_limit_bytes=vmem * 1024 * 1024),
    )(*args, *after)


def begin(x_ref, cot_ref, second_ref, xt_ref, out_ref, x_in, cot_in, pad_ref, sems):
    x_copy = pltpu.make_async_copy(x_ref, x_in, sems.at[0])
    cot_copy = pltpu.make_async_copy(cot_ref, cot_in, sems.at[1])
    x_copy.start()
    cot_copy.start()
    pad_ref[...] = jnp.zeros(pad_ref.shape, F32)
    eye = ones_where(iota((KCH, KCH), 0) == iota((KCH, KCH), 1))
    pad_ref[0:KCH, 0:64] = dot(eye, second_ref[...], NT)
    more = jnp.concatenate([pltpu.roll(pad_ref[16:24, :], 64, 1), jnp.zeros((8, HALF), F32)], axis=0)
    tile = (pad_ref[0:16, :] + more).astype(BF)
    out_ref[CS:CS + 16, :] = jnp.concatenate([tile] * 4, axis=1)
    x_copy.wait()
    zeros = jnp.zeros((W - CS, BLK), F32)
    xt = jnp.concatenate([x_in[...].astype(F32), zeros], axis=0).T
    xt_ref[...] = xt.reshape(NB, 8, W).astype(BF)
    cot_copy.wait()
    out_ref[0:CS, :] = cot_in[...]


def prepare(gain_ref, bias_ref, cross_ref, gain_out_ref, bias_out_ref, kron_ref, kront_ref, pad_ref):
    for row, out_ref in ((gain_ref, gain_out_ref), (bias_ref, bias_out_ref)):
        pad_ref[...] = jnp.zeros(pad_ref.shape, F32)
        pad_ref[:, 0:CS] = jnp.broadcast_to(row[...], (HALF, CS))
        out_ref[...] = pad_ref[...].T[:CS]
    spread = ones_where(iota((BLK, NB), 0) // 8 == iota((BLK, NB), 1))
    same = iota((BLK, BLK), 0) % 8 == iota((BLK, BLK), 1) % 8
    half = dot(spread, cross_ref[...], NN).astype(BF)
    kron_ref[...] = jnp.where(same, dot(half, spread, NT), 0.0).astype(BF)
    half = dot(spread, cross_ref[...], NT).astype(BF)
    kront_ref[...] = jnp.where(same, dot(half, spread, NT), 0.0).astype(BF)


def cross_forward(kront_ref, cols_ref, out_ref):
    cols = cols_ref[...].astype(F32).reshape(BLK, W).astype(BF)
    out_ref[...] = dot(kront_ref[...], cols).reshape(NB, 8, W).astype(BF)


def forward(u_ref, block_ref, x_ref, gain_ref, bias_ref, weight_ref,
            mixed_ref, gate_ref, hidden_ref, act_ref, slope_ref):
    u = u_ref[...].astype(F32).reshape(BLK, W).astype(BF)
    mixed = dot(u, block_ref[...], TN)[:CS].astype(BF)
    mixed_ref[...] = mixed
    x = x_ref[...].astype(F32)
    gain = jnp.concatenate([gain_ref[...]] * 4, axis=1)
    bias = jnp.concatenate([bias_ref[...]] * 4, axis=1)
    gate = jax.nn.sigmoid(x * gain + bias)
    gate_ref[...] = gate
    hidden = (x + gate * mixed.astype(F32)).astype(BF)
    hidden_ref[...] = hidden
    pre = dot(weight_ref[0], hidden)
    root = 0.7978845608028654
    square = pre * pre
    curve = jnp.tanh(root * (pre + 0.044715 * (square * pre)))
    act_ref[...] = (pre * (0.5 * (1.0 + curve))).astype(BF)
    slope_ref[...] = 0.5 * (1.0 + curve) + pre * (0.5 * (1.0 - curve * curve)) * (
        root * (1.0 + (3 * 0.044715) * square)
    )


def channel(u_ref, block_ref, x_ref, gain_ref, weight_ref, mixed_ref, gate_ref, hidden_ref, act_ref,
            slope_ref, cot_ref, cots_ref, flag_ref, send_ref, rest_ref, factor_ref):
    q = flag_ref[0]
    act = act_ref[...].astype(F32)
    tiles = jnp.concatenate([cots_ref[g, CS:CS + 16, 0:HALF].astype(F32) for g in range(CB)], axis=0).astype(BF)
    k, m = iota((CS, HALF), 0), iota((CS, HALF), 1)
    start = KCH * (m // 16)
    low = dot(ones_where(k == start + m % 16), tiles)
    high = dot(ones_where((k == start + 16 + m % 16) & (m % 16 < 4)), tiles)
    second = jnp.where(m < 64, low + pltpu.roll(high, 64, 1), 0.0).astype(BF)
    pair, group = iota((HALF, HALF), 0), iota((HALF, HALF), 1)
    factor_ref[...] = dot(second, ones_where((pair == q * CB + group) & (group < CB)))
    back = dot(second, ones_where((pair == group * CB + q) & (group < CB)))
    d_act = jnp.zeros((CS, BLK), F32)
    grad_second = jnp.zeros((CS, HALF), F32)
    for g in range(CB):
        cot = cots_ref[g, 0:CS, :].astype(F32)
        d_act = d_act + back[:, g:g + 1] * cot
        column = jnp.sum(cot * act, axis=1, keepdims=True)
        grad_second = jnp.where(m == 32 + CB * g + q, column, grad_second)
    d_pre = (d_act.astype(BF).astype(F32) * slope_ref[...]).astype(BF)
    zeros = jnp.zeros((W - CS, BLK), F32)
    tall = jnp.concatenate([hidden_ref[...].astype(F32), zeros], axis=0).astype(BF)
    grad_first = dot(d_pre, tall, NT)
    d_hidden = cot_ref[...].astype(F32) + dot(weight_ref[0], d_pre, TN)
    gate = gate_ref[...]
    d_mixed = jnp.concatenate([d_hidden * gate, zeros], axis=0).astype(BF)
    d_gate = d_hidden * mixed_ref[...].astype(F32) * gate * (1.0 - gate)
    grad_gain = jnp.sum(d_gate * x_ref[...].astype(F32), axis=1, keepdims=True)
    grad_bias = jnp.sum(d_gate, axis=1, keepdims=True)
    gain = jnp.concatenate([gain_ref[...]] * 4, axis=1)
    rest_ref[...] = d_hidden + d_gate * gain
    v = dot(block_ref[...], d_mixed, NT)
    left, right = grad_first[:, :HALF], grad_first[:, HALF:]
    misc_b = jnp.where(m < 64, pltpu.roll(left, 32, 1), pltpu.roll(right, 64, 1))
    misc_b = jnp.where(m == 96, grad_gain, jnp.where(m == 97, grad_bias, misc_b))
    misc = jnp.concatenate([left, misc_b, grad_second, jnp.zeros((32, HALF), F32)], axis=0)
    right = jnp.where(iota((BLK, HALF), 1) < 32, v[:, HALF:], misc).reshape(NB, 8, HALF)
    left = v[:, :HALF].reshape(NB, 8, HALF)
    send_ref[:, 0:16, :] = jnp.concatenate([left, right], axis=1).astype(BF)
    u = u_ref[...].astype(F32).reshape(BLK, W).astype(BF)
    d_block = dot(u, d_mixed, NN)
    parts = [d_block[:, HALF * s:HALF * (s + 1)].reshape(NB, 8, HALF) for s in range(4)]
    send_ref[:, 16:48, :] = jnp.concatenate(parts, axis=1).astype(BF)


def cross_backward(recv_ref, x_ref, kron_ref, act_ref, send_ref, d_input_ref, misc_ref, pass_ref):
    pass_ref[...] = act_ref[...]
    head = recv_ref[:, 0:16, :].astype(F32)
    low = iota((NB, 8, HALF), 2) < 32
    left, right = head[:, 0:8, :], head[:, 8:16, :]
    v = jnp.concatenate(
        [left.reshape(BLK, HALF), jnp.where(low, right, 0.0).reshape(BLK, HALF)], axis=1
    ).astype(BF)
    misc = jnp.sum(right, axis=0)
    misc_ref[...] = misc
    d_input_ref[...] = dot(kron_ref[...], v).astype(BF)
    x = x_ref[...].astype(F32).reshape(BLK, W).astype(BF)
    pairs = dot(x, v, NT)
    same = iota((BLK, BLK), 0) % 8 == iota((BLK, BLK), 1) % 8
    rows = jnp.sum(jnp.where(same, pairs, 0.0).reshape(NB, 8, BLK), axis=1)
    high = rows.astype(BF)
    rest = (rows - high.astype(F32)).astype(BF)
    at, lane = iota((BLK, HALF), 0) // 8, iota((BLK, HALF), 1)
    cross = jnp.zeros((32, HALF), F32)
    for s in range(2):
        gather = ones_where(at == lane - 64 * s)
        cross = cross + dot(high[32 * s:32 * s + 32], gather) + dot(rest[32 * s:32 * s + 32], gather)
    tail = jnp.sum(recv_ref[:, 16:48, :].astype(F32), axis=0)
    send_ref[...] = jnp.concatenate([tail, cross, misc], axis=0)


def pack_last(recv_ref, own_ref, d_input_ref, flag_ref, send_ref):
    total = jnp.sum(recv_ref[...], axis=0)
    misc = jnp.where(flag_ref[3] > 0, total[64:72], own_ref[...])
    d_input = d_input_ref[...].astype(F32)
    left = d_input[:, :HALF].reshape(NB, 8, HALF)
    right = jnp.where(
        iota((NB, 8, HALF), 2) < 32, d_input[:, HALF:].reshape(NB, 8, HALF), misc[None]
    )
    send_ref[:, 0:16, :] = jnp.concatenate([left, right], axis=1).astype(BF)
    first = flag_ref[2] == 0
    block = jnp.where(first, total[0:16], total[16:32])
    cross = jnp.where(first, total[32:48], total[48:64])
    tail = jnp.concatenate([block, cross], axis=0).astype(BF)
    send_ref[:, 16:48, :] = jnp.broadcast_to(tail[None], (NB, 32, HALF))


def split_last(recv_ref, out_ref):
    recv = recv_ref[:, 16:32, :].astype(F32)
    left = recv[:, 0:8, :].reshape(BLK, HALF)
    right = recv[:, 8:16, :].reshape(BLK, HALF)
    out_ref[0:BLK, :] = jnp.concatenate([left, right], axis=1).astype(BF)
    cross = jnp.sum(recv_ref[:, 32:48, :].astype(F32), axis=0)
    out_ref[BLK:BLK + 16, :] = jnp.concatenate([cross, cross], axis=1).astype(BF)


def finish_output(hidden_ref, factor_ref, acts_ref, out_ref):
    factor = factor_ref[...]
    branch = jnp.zeros((CS, BLK), F32)
    for g in range(CB):
        branch = branch + factor[:, g:g + 1] * acts_ref[g].astype(F32)
    out_ref[...] = (hidden_ref[...].astype(F32) + branch.astype(BF).astype(F32)).astype(BF)


def finish_input(recv_ref, rest_ref, flag_ref, grad_ref, first_ref, second_ref, gain_ref, bias_ref):
    head = recv_ref[:, 0:16, :].astype(F32)
    left, misc = head[:, 0:8, :], head[:, 8:16, :].reshape(BLK, HALF)
    low = iota((BLK, HALF), 1) < 32
    d_input = jnp.concatenate([left.reshape(BLK, HALF), jnp.where(low, misc, 0.0)], axis=1)
    grad_ref[...] = (rest_ref[...] + d_input.T[:CS]).astype(BF)
    a, b = misc[0:CS], misc[CS:2 * CS]
    first_ref[0, :, 0:HALF] = jnp.where(iota((CS, HALF), 1) >= 32, a, pltpu.roll(b, 96, 1))
    first_ref[0, :, HALF:CS] = pltpu.roll(b, 64, 1)[:, 0:32]
    rows = misc[CS:CS + W].T
    gain_ref[...] = rows[96:97, 0:CS]
    bias_ref[...] = rows[97:98, 0:CS]
    pick = ones_where(iota((CS, KCH), 0) == iota((CS, KCH), 1) + KCH * flag_ref[0])
    second_ref[...] = dot(misc[2 * CS:3 * CS].astype(BF), pick, TN)[32:96]


def finish_sums(own_ref, swap_ref, flag_ref, block_ref, cross_ref):
    first = flag_ref[2] == 0
    own, swap = own_ref[...].astype(F32), swap_ref[...].astype(F32)
    low, high = jnp.where(first, own, swap), jnp.where(first, swap, own)
    block_ref[:, 0:W] = low[0:BLK]
    block_ref[:, W:BLK] = high[0:BLK]
    cross = jnp.concatenate([low[BLK:, 0:HALF], high[BLK:, 0:HALF]], axis=0)
    cross_ref[0:32, :] = cross[:, 0:64]
    cross_ref[32:64, :] = pltpu.roll(cross, 64, 1)[:, 0:64]


PAIR = [(i, i ^ 1) for i in range(CB)]


def on_device(layer_input, w_block, w_cross, ch_first, ch_second, gate_gain, gate_bias, cotangent):
    swap = functools.partial(lax.all_to_all, split_axis=0, concat_axis=0, tiled=True)
    ctx, ch = lax.axis_index("ctx"), lax.axis_index("ch")
    second_sum = (ctx >= 40) & (ctx < 60)
    flag = jnp.stack([ch, ch // 2, ch % 2, second_sum.astype(jnp.int32)]).astype(jnp.int32)
    xt, packed = call(
        begin, [((NB, 8, W), BF), ((CS + 16, BLK), BF)],
        layer_input, cotangent, ch_second.transpose(1, 2, 0).reshape(CB * CB, KCH),
        scratch=[pltpu.VMEM((CS, BLK), BF), pltpu.VMEM((CS, BLK), BF), pltpu.VMEM((24, HALF), F32),
                 pltpu.SemaphoreType.DMA((2,))],
        far=(0, 1), vmem=60,
    )
    x_cols = swap(xt, "ctx")
    cots = lax.all_gather(packed, "ch")
    gain, bias, kron, kront = call(
        prepare,
        [((CS, HALF), F32), ((CS, HALF), F32), ((BLK, BLK), BF), ((BLK, BLK), BF)],
        gate_gain.reshape(1, CS), gate_bias.reshape(1, CS), w_cross,
        scratch=[pltpu.VMEM((HALF, W), F32)],
    )
    (u_cols,) = call(cross_forward, [((NB, 8, W), BF)], kront, x_cols)
    u = swap(u_cols, "ctx")
    wide = (CS, BLK)
    mixed, gate, hidden, act, slope = call(
        forward, [(wide, BF), (wide, F32), (wide, BF), (wide, BF), (wide, F32)],
        u, w_block, layer_input, gain, bias, ch_first,
    )
    send, rest, factor = call(
        channel, [((NB, 48, HALF), BF), (wide, F32), ((CS, HALF), F32)],
        u, w_block, layer_input, gain, ch_first, mixed, gate, hidden, act, slope, cotangent, cots, flag,
        smem=(12,),
    )
    recv = swap(send, "ctx")
    send, d_input, misc, act = call(
        cross_backward,
        [((72, HALF), F32), ((BLK, W), BF), ((8, HALF), F32), ((CS, BLK), BF)],
        recv, x_cols, kron, act,
    )
    acts = lax.all_gather(act, "ch")
    (send,) = call(
        pack_last, [((NB, 48, HALF), BF)], lax.all_gather(send, "ch"), misc, d_input, flag, smem=(3,)
    )
    recv = swap(send, "ctx")
    (half,) = call(split_last, [((BLK + 16, W), BF)], recv)
    swapped = lax.ppermute(half, "ch", PAIR)
    grad_input, grad_first, grad_second, grad_gain, grad_bias = call(
        finish_input,
        [((CS, BLK), BF), ((1, CS, CS), F32), ((CB * CB, KCH), F32), ((1, CS), F32), ((1, CS), F32)],
        recv, rest, flag,
        smem=(2,),
    )
    (output,) = call(finish_output, [((CS, BLK), BF)], hidden, factor, acts, after=[half])
    grad_block, grad_cross = call(
        finish_sums, [((BLK, BLK), F32), ((NB, NB), F32)], half, swapped, flag, smem=(2,)
    )
    return (
        output,
        grad_input,
        grad_block,
        grad_cross,
        grad_first,
        grad_second.reshape(CB, CB, KCH).transpose(2, 0, 1),
        grad_gain.reshape(CS),
        grad_bias.reshape(CS),
    )


def solution(mesh):
    in_specs = (
        P("ch", "ctx"),
        P(),
        P(),
        P("ch", None, None),
        P("ch", None, None),
        P("ch"),
        P("ch"),
        P("ch", "ctx"),
    )
    out_specs = (
        P("ch", "ctx"),
        P("ch", "ctx"),
        P(),
        P(),
        P("ch", None, None),
        P("ch", None, None),
        P("ch"),
        P("ch"),
    )
    return jax.shard_map(
        on_device, mesh=mesh, in_specs=in_specs, out_specs=out_specs, check_vma=False
    )
```

```python
import functools

import jax
import jax.numpy as jnp
from jax import lax
from jax.experimental import pallas as pl
from jax.experimental.pallas import tpu as pltpu
from jax.sharding import PartitionSpec as P

BF = jnp.bfloat16
F32 = jnp.float32
NB = 64
BLK = 512
CB = 8
CS = 160
KCH = 20
W = 256
HALF = 128


def dot(a, b, dims=((1,), (0,))):
    return lax.dot_general(a, b, (dims, ((), ())), preferred_element_type=F32)


NN = ((1,), (0,))
NT = ((1,), (1,))
TN = ((0,), (0,))


def iota(shape, axis):
    return lax.broadcasted_iota(jnp.int32, shape, axis)


def ones_where(cond):
    return jnp.where(cond, 1.0, 0.0).astype(BF)


def call(body, out_shapes, *args, scratch=(), smem=(), far=(), vmem=48, after=()):
    specs = [
        pl.BlockSpec(
            memory_space=pltpu.SMEM if at in smem else pl.ANY if at in far else pltpu.VMEM
        )
        for at in range(len(args))
    ]
    specs += [pl.BlockSpec(memory_space=pl.ANY) for _ in after]
    used, held = len(args), len(args) + len(after)

    def run(*refs):
        body(*refs[:used], *refs[held:])

    return pl.pallas_call(
        run,
        out_shape=[jax.ShapeDtypeStruct(s, d) for s, d in out_shapes],
        in_specs=specs,
        out_specs=[pl.BlockSpec(memory_space=pltpu.VMEM) for _ in out_shapes],
        scratch_shapes=list(scratch),
        compiler_params=pltpu.CompilerParams(vmem_limit_bytes=vmem * 1024 * 1024),
    )(*args, *after)


def pack_cotangent(cot_ref, second_ref, out_ref, cot_in, pad_ref, sem):
    copy = pltpu.make_async_copy(cot_ref, cot_in, sem)
    copy.start()
    pad_ref[...] = jnp.zeros(pad_ref.shape, F32)
    eye = ones_where(iota((KCH, KCH), 0) == iota((KCH, KCH), 1))
    pad_ref[0:KCH, 0:64] = dot(eye, second_ref[...], NT)
    more = jnp.concatenate([pltpu.roll(pad_ref[16:24, :], 64, 1), jnp.zeros((8, HALF), F32)], axis=0)
    tile = (pad_ref[0:16, :] + more).astype(BF)
    out_ref[CS:CS + 16, :] = jnp.concatenate([tile] * 4, axis=1)
    copy.wait()
    out_ref[0:CS, :] = cot_in[...]


def transpose_input(x_ref, xt_ref, x_in, sem):
    copy = pltpu.make_async_copy(x_ref, x_in, sem)
    copy.start()
    copy.wait()
    zeros = jnp.zeros((W - CS, BLK), F32)
    xt = jnp.concatenate([x_in[...].astype(F32), zeros], axis=0).T
    xt_ref[...] = xt.reshape(NB, 8, W).astype(BF)


def prepare(gain_ref, bias_ref, cross_ref, gain_out_ref, bias_out_ref, kron_ref, kront_ref, pad_ref):
    for row, out_ref in ((gain_ref, gain_out_ref), (bias_ref, bias_out_ref)):
        pad_ref[...] = jnp.zeros(pad_ref.shape, F32)
        pad_ref[:, 0:CS] = jnp.broadcast_to(row[...], (HALF, CS))
        out_ref[...] = pad_ref[...].T[:CS]
    spread = ones_where(iota((BLK, NB), 0) // 8 == iota((BLK, NB), 1))
    same = iota((BLK, BLK), 0) % 8 == iota((BLK, BLK), 1) % 8
    half = dot(spread, cross_ref[...], NN).astype(BF)
    kron_ref[...] = jnp.where(same, dot(half, spread, NT), 0.0).astype(BF)
    half = dot(spread, cross_ref[...], NT).astype(BF)
    kront_ref[...] = jnp.where(same, dot(half, spread, NT), 0.0).astype(BF)


def cross_forward(kront_ref, cols_ref, out_ref):
    cols = cols_ref[...].astype(F32).reshape(BLK, W).astype(BF)
    out_ref[...] = dot(kront_ref[...], cols).reshape(NB, 8, W).astype(BF)


def forward(u_ref, block_ref, x_ref, gain_ref, bias_ref, weight_ref,
            mixed_ref, gate_ref, hidden_ref, act_ref, slope_ref):
    u = u_ref[...].astype(F32).reshape(BLK, W).astype(BF)
    mixed = dot(u, block_ref[...], TN)[:CS].astype(BF)
    mixed_ref[...] = mixed
    x = x_ref[...].astype(F32)
    gain = jnp.concatenate([gain_ref[...]] * 4, axis=1)
    bias = jnp.concatenate([bias_ref[...]] * 4, axis=1)
    gate = jax.nn.sigmoid(x * gain + bias)
    gate_ref[...] = gate
    hidden = (x + gate * mixed.astype(F32)).astype(BF)
    hidden_ref[...] = hidden
    pre = dot(weight_ref[0], hidden)
    root = 0.7978845608028654
    square = pre * pre
    curve = jnp.tanh(root * (pre + 0.044715 * (square * pre)))
    act_ref[...] = (pre * (0.5 * (1.0 + curve))).astype(BF)
    slope_ref[...] = 0.5 * (1.0 + curve) + pre * (0.5 * (1.0 - curve * curve)) * (
        root * (1.0 + (3 * 0.044715) * square)
    )


def channel(u_ref, block_ref, x_ref, gain_ref, weight_ref, mixed_ref, gate_ref, hidden_ref, act_ref,
            slope_ref, cot_ref, cots_ref, flag_ref, send_ref, rest_ref, factor_ref):
    q = flag_ref[0]
    act = act_ref[...].astype(F32)
    tiles = jnp.concatenate([cots_ref[g, CS:CS + 16, 0:HALF].astype(F32) for g in range(CB)], axis=0).astype(BF)
    k, m = iota((CS, HALF), 0), iota((CS, HALF), 1)
    start = KCH * (m // 16)
    low = dot(ones_where(k == start + m % 16), tiles)
    high = dot(ones_where((k == start + 16 + m % 16) & (m % 16 < 4)), tiles)
    second = jnp.where(m < 64, low + pltpu.roll(high, 64, 1), 0.0).astype(BF)
    pair, group = iota((HALF, HALF), 0), iota((HALF, HALF), 1)
    factor_ref[...] = dot(second, ones_where((pair == q * CB + group) & (group < CB)))
    back = dot(second, ones_where((pair == group * CB + q) & (group < CB)))
    d_act = jnp.zeros((CS, BLK), F32)
    grad_second = jnp.zeros((CS, HALF), F32)
    for g in range(CB):
        cot = cots_ref[g, 0:CS, :].astype(F32)
        d_act = d_act + back[:, g:g + 1] * cot
        column = jnp.sum(cot * act, axis=1, keepdims=True)
        grad_second = jnp.where(m == 32 + CB * g + q, column, grad_second)
    d_pre = (d_act.astype(BF).astype(F32) * slope_ref[...]).astype(BF)
    zeros = jnp.zeros((W - CS, BLK), F32)
    tall = jnp.concatenate([hidden_ref[...].astype(F32), zeros], axis=0).astype(BF)
    grad_first = dot(d_pre, tall, NT)
    d_hidden = cot_ref[...].astype(F32) + dot(weight_ref[0], d_pre, TN)
    gate = gate_ref[...]
    d_mixed = jnp.concatenate([d_hidden * gate, zeros], axis=0).astype(BF)
    d_gate = d_hidden * mixed_ref[...].astype(F32) * gate * (1.0 - gate)
    grad_gain = jnp.sum(d_gate * x_ref[...].astype(F32), axis=1, keepdims=True)
    grad_bias = jnp.sum(d_gate, axis=1, keepdims=True)
    gain = jnp.concatenate([gain_ref[...]] * 4, axis=1)
    rest_ref[...] = d_hidden + d_gate * gain
    v = dot(block_ref[...], d_mixed, NT)
    left, right = grad_first[:, :HALF], grad_first[:, HALF:]
    misc_b = jnp.where(m < 64, pltpu.roll(left, 32, 1), pltpu.roll(right, 64, 1))
    misc_b = jnp.where(m == 96, grad_gain, jnp.where(m == 97, grad_bias, misc_b))
    misc = jnp.concatenate([left, misc_b, grad_second, jnp.zeros((32, HALF), F32)], axis=0)
    right = jnp.where(iota((BLK, HALF), 1) < 32, v[:, HALF:], misc).reshape(NB, 8, HALF)
    left = v[:, :HALF].reshape(NB, 8, HALF)
    send_ref[:, 0:16, :] = jnp.concatenate([left, right], axis=1).astype(BF)
    u = u_ref[...].astype(F32).reshape(BLK, W).astype(BF)
    d_block = dot(u, d_mixed, NN)
    parts = [d_block[:, HALF * s:HALF * (s + 1)].reshape(NB, 8, HALF) for s in range(4)]
    send_ref[:, 16:48, :] = jnp.concatenate(parts, axis=1).astype(BF)


def cross_backward(recv_ref, x_ref, kron_ref, act_ref, send_ref, d_input_ref, misc_ref, pass_ref):
    pass_ref[...] = act_ref[...]
    head = recv_ref[:, 0:16, :].astype(F32)
    low = iota((NB, 8, HALF), 2) < 32
    left, right = head[:, 0:8, :], head[:, 8:16, :]
    v = jnp.concatenate(
        [left.reshape(BLK, HALF), jnp.where(low, right, 0.0).reshape(BLK, HALF)], axis=1
    ).astype(BF)
    misc = jnp.sum(right, axis=0)
    misc_ref[...] = misc
    d_input_ref[...] = dot(kron_ref[...], v).astype(BF)
    x = x_ref[...].astype(F32).reshape(BLK, W).astype(BF)
    pairs = dot(x, v, NT)
    same = iota((BLK, BLK), 0) % 8 == iota((BLK, BLK), 1) % 8
    rows = jnp.sum(jnp.where(same, pairs, 0.0).reshape(NB, 8, BLK), axis=1)
    high = rows.astype(BF)
    rest = (rows - high.astype(F32)).astype(BF)
    at, lane = iota((BLK, HALF), 0) // 8, iota((BLK, HALF), 1)
    cross = jnp.zeros((32, HALF), F32)
    for s in range(2):
        gather = ones_where(at == lane - 64 * s)
        cross = cross + dot(high[32 * s:32 * s + 32], gather) + dot(rest[32 * s:32 * s + 32], gather)
    tail = jnp.sum(recv_ref[:, 16:48, :].astype(F32), axis=0)
    send_ref[...] = jnp.concatenate([tail, cross, misc], axis=0)


def pack_last(recv_ref, own_ref, d_input_ref, flag_ref, send_ref):
    total = jnp.sum(recv_ref[...], axis=0)
    misc = jnp.where(flag_ref[3] > 0, total[64:72], own_ref[...])
    d_input = d_input_ref[...].astype(F32)
    left = d_input[:, :HALF].reshape(NB, 8, HALF)
    right = jnp.where(
        iota((NB, 8, HALF), 2) < 32, d_input[:, HALF:].reshape(NB, 8, HALF), misc[None]
    )
    send_ref[:, 0:16, :] = jnp.concatenate([left, right], axis=1).astype(BF)
    first = flag_ref[2] == 0
    block = jnp.where(first, total[0:16], total[16:32])
    cross = jnp.where(first, total[32:48], total[48:64])
    tail = jnp.concatenate([block, cross], axis=0).astype(BF)
    send_ref[:, 16:48, :] = jnp.broadcast_to(tail[None], (NB, 32, HALF))


def split_last(recv_ref, out_ref):
    recv = recv_ref[:, 16:32, :].astype(F32)
    left = recv[:, 0:8, :].reshape(BLK, HALF)
    right = recv[:, 8:16, :].reshape(BLK, HALF)
    out_ref[0:BLK, :] = jnp.concatenate([left, right], axis=1).astype(BF)
    cross = jnp.sum(recv_ref[:, 32:48, :].astype(F32), axis=0)
    out_ref[BLK:BLK + 16, :] = jnp.concatenate([cross, cross], axis=1).astype(BF)


def finish_output(hidden_ref, factor_ref, acts_ref, out_ref):
    factor = factor_ref[...]
    branch = jnp.zeros((CS, BLK), F32)
    for g in range(CB):
        branch = branch + factor[:, g:g + 1] * acts_ref[g].astype(F32)
    out_ref[...] = (hidden_ref[...].astype(F32) + branch.astype(BF).astype(F32)).astype(BF)


def finish_input(recv_ref, rest_ref, flag_ref, grad_ref, first_ref, second_ref, gain_ref, bias_ref):
    head = recv_ref[:, 0:16, :].astype(F32)
    left, misc = head[:, 0:8, :], head[:, 8:16, :].reshape(BLK, HALF)
    low = iota((BLK, HALF), 1) < 32
    d_input = jnp.concatenate([left.reshape(BLK, HALF), jnp.where(low, misc, 0.0)], axis=1)
    grad_ref[...] = (rest_ref[...] + d_input.T[:CS]).astype(BF)
    a, b = misc[0:CS], misc[CS:2 * CS]
    first_ref[0, :, 0:HALF] = jnp.where(iota((CS, HALF), 1) >= 32, a, pltpu.roll(b, 96, 1))
    first_ref[0, :, HALF:CS] = pltpu.roll(b, 64, 1)[:, 0:32]
    rows = misc[CS:CS + W].T
    gain_ref[...] = rows[96:97, 0:CS]
    bias_ref[...] = rows[97:98, 0:CS]
    pick = ones_where(iota((CS, KCH), 0) == iota((CS, KCH), 1) + KCH * flag_ref[0])
    second_ref[...] = dot(misc[2 * CS:3 * CS].astype(BF), pick, TN)[32:96]


def finish_sums(own_ref, swap_ref, flag_ref, block_ref, cross_ref):
    first = flag_ref[2] == 0
    own, swap = own_ref[...].astype(F32), swap_ref[...].astype(F32)
    low, high = jnp.where(first, own, swap), jnp.where(first, swap, own)
    block_ref[:, 0:W] = low[0:BLK]
    block_ref[:, W:BLK] = high[0:BLK]
    cross = jnp.concatenate([low[BLK:, 0:HALF], high[BLK:, 0:HALF]], axis=0)
    cross_ref[0:32, :] = cross[:, 0:64]
    cross_ref[32:64, :] = pltpu.roll(cross, 64, 1)[:, 0:64]


PAIR = [(i, i ^ 1) for i in range(CB)]


def on_device(layer_input, w_block, w_cross, ch_first, ch_second, gate_gain, gate_bias, cotangent):
    swap = functools.partial(lax.all_to_all, split_axis=0, concat_axis=0, tiled=True)
    ctx, ch = lax.axis_index("ctx"), lax.axis_index("ch")
    second_sum = (ctx >= 40) & (ctx < 60)
    flag = jnp.stack([ch, ch // 2, ch % 2, second_sum.astype(jnp.int32)]).astype(jnp.int32)
    (packed,) = call(
        pack_cotangent, [((CS + 16, BLK), BF)],
        cotangent, ch_second.transpose(1, 2, 0).reshape(CB * CB, KCH),
        scratch=[pltpu.VMEM((CS, BLK), BF), pltpu.VMEM((24, HALF), F32), pltpu.SemaphoreType.DMA],
        far=(0,), vmem=60,
    )
    (xt,) = call(
        transpose_input, [((NB, 8, W), BF)], layer_input,
        scratch=[pltpu.VMEM((CS, BLK), BF), pltpu.SemaphoreType.DMA],
        far=(0,), vmem=60, after=[packed],
    )
    x_cols = swap(xt, "ctx")
    cots = lax.all_gather(packed, "ch")
    gain, bias, kron, kront = call(
        prepare,
        [((CS, HALF), F32), ((CS, HALF), F32), ((BLK, BLK), BF), ((BLK, BLK), BF)],
        gate_gain.reshape(1, CS), gate_bias.reshape(1, CS), w_cross,
        scratch=[pltpu.VMEM((HALF, W), F32)],
    )
    (u_cols,) = call(cross_forward, [((NB, 8, W), BF)], kront, x_cols)
    u = swap(u_cols, "ctx")
    wide = (CS, BLK)
    mixed, gate, hidden, act, slope = call(
        forward, [(wide, BF), (wide, F32), (wide, BF), (wide, BF), (wide, F32)],
        u, w_block, layer_input, gain, bias, ch_first,
    )
    send, rest, factor = call(
        channel, [((NB, 48, HALF), BF), (wide, F32), ((CS, HALF), F32)],
        u, w_block, layer_input, gain, ch_first, mixed, gate, hidden, act, slope, cotangent, cots, flag,
        smem=(12,),
    )
    recv = swap(send, "ctx")
    send, d_input, misc, act = call(
        cross_backward,
        [((72, HALF), F32), ((BLK, W), BF), ((8, HALF), F32), ((CS, BLK), BF)],
        recv, x_cols, kron, act,
    )
    acts = lax.all_gather(act, "ch")
    (send,) = call(
        pack_last, [((NB, 48, HALF), BF)], lax.all_gather(send, "ch"), misc, d_input, flag, smem=(3,)
    )
    recv = swap(send, "ctx")
    (half,) = call(split_last, [((BLK + 16, W), BF)], recv)
    swapped = lax.ppermute(half, "ch", PAIR)
    grad_input, grad_first, grad_second, grad_gain, grad_bias = call(
        finish_input,
        [((CS, BLK), BF), ((1, CS, CS), F32), ((CB * CB, KCH), F32), ((1, CS), F32), ((1, CS), F32)],
        recv, rest, flag,
        smem=(2,),
    )
    (output,) = call(finish_output, [((CS, BLK), BF)], hidden, factor, acts, after=[half])
    grad_block, grad_cross = call(
        finish_sums, [((BLK, BLK), F32), ((NB, NB), F32)], half, swapped, flag, smem=(2,)
    )
    return (
        output,
        grad_input,
        grad_block,
        grad_cross,
        grad_first,
        grad_second.reshape(CB, CB, KCH).transpose(2, 0, 1),
        grad_gain.reshape(CS),
        grad_bias.reshape(CS),
    )


def solution(mesh):
    in_specs = (
        P("ch", "ctx"),
        P(),
        P(),
        P("ch", None, None),
        P("ch", None, None),
        P("ch"),
        P("ch"),
        P("ch", "ctx"),
    )
    out_specs = (
        P("ch", "ctx"),
        P("ch", "ctx"),
        P(),
        P(),
        P("ch", None, None),
        P("ch", None, None),
        P("ch"),
        P("ch"),
    )
    return jax.shard_map(
        on_device, mesh=mesh, in_specs=in_specs, out_specs=out_specs, check_vma=False
    )
```

```python
import functools

import jax
import jax.numpy as jnp
from jax import lax
from jax.experimental import pallas as pl
from jax.experimental.pallas import tpu as pltpu
from jax.sharding import PartitionSpec as P

BF = jnp.bfloat16
F32 = jnp.float32
NB = 64
BLK = 512
CB = 8
CS = 160
KCH = 20
W = 256
HALF = 128


def dot(a, b, dims=((1,), (0,))):
    return lax.dot_general(a, b, (dims, ((), ())), preferred_element_type=F32)


NN = ((1,), (0,))
NT = ((1,), (1,))
TN = ((0,), (0,))


def iota(shape, axis):
    return lax.broadcasted_iota(jnp.int32, shape, axis)


def ones_where(cond):
    return jnp.where(cond, 1.0, 0.0).astype(BF)


def call(body, out_shapes, *args, scratch=(), smem=(), far=(), vmem=48, after=()):
    specs = [
        pl.BlockSpec(
            memory_space=pltpu.SMEM if at in smem else pl.ANY if at in far else pltpu.VMEM
        )
        for at in range(len(args))
    ]
    specs += [pl.BlockSpec(memory_space=pl.ANY) for _ in after]
    used, held = len(args), len(args) + len(after)

    def run(*refs):
        body(*refs[:used], *refs[held:])

    return pl.pallas_call(
        run,
        out_shape=[jax.ShapeDtypeStruct(s, d) for s, d in out_shapes],
        in_specs=specs,
        out_specs=[pl.BlockSpec(memory_space=pltpu.VMEM) for _ in out_shapes],
        scratch_shapes=list(scratch),
        compiler_params=pltpu.CompilerParams(vmem_limit_bytes=vmem * 1024 * 1024),
    )(*args, *after)


def begin(x_ref, cot_ref, second_ref, xt_ref, out_ref, x_in, cot_in, pad_ref, sems):
    x_copy = pltpu.make_async_copy(x_ref, x_in, sems.at[0])
    cot_copy = pltpu.make_async_copy(cot_ref, cot_in, sems.at[1])
    x_copy.start()
    cot_copy.start()
    pad_ref[...] = jnp.zeros(pad_ref.shape, F32)
    eye = ones_where(iota((KCH, KCH), 0) == iota((KCH, KCH), 1))
    pad_ref[0:KCH, 0:64] = dot(eye, second_ref[...], NT)
    more = jnp.concatenate([pltpu.roll(pad_ref[16:24, :], 64, 1), jnp.zeros((8, HALF), F32)], axis=0)
    tile = (pad_ref[0:16, :] + more).astype(BF)
    out_ref[CS:CS + 16, :] = jnp.concatenate([tile] * 4, axis=1)
    x_copy.wait()
    zeros = jnp.zeros((W - CS, BLK), F32)
    xt = jnp.concatenate([x_in[...].astype(F32), zeros], axis=0).T
    xt_ref[...] = xt.reshape(NB, 8, W).astype(BF)
    cot_copy.wait()
    out_ref[0:CS, :] = cot_in[...]


def prepare(gain_ref, bias_ref, cross_ref, gain_out_ref, bias_out_ref, kron_ref, kront_ref, pad_ref):
    for row, out_ref in ((gain_ref, gain_out_ref), (bias_ref, bias_out_ref)):
        pad_ref[...] = jnp.zeros(pad_ref.shape, F32)
        pad_ref[:, 0:CS] = jnp.broadcast_to(row[...], (HALF, CS))
        out_ref[...] = pad_ref[...].T[:CS]
    spread = ones_where(iota((BLK, NB), 0) // 8 == iota((BLK, NB), 1))
    same = iota((BLK, BLK), 0) % 8 == iota((BLK, BLK), 1) % 8
    half = dot(spread, cross_ref[...], NN).astype(BF)
    kron_ref[...] = jnp.where(same, dot(half, spread, NT), 0.0).astype(BF)
    half = dot(spread, cross_ref[...], NT).astype(BF)
    kront_ref[...] = jnp.where(same, dot(half, spread, NT), 0.0).astype(BF)


def cross_forward(kront_ref, cols_ref, out_ref):
    cols = cols_ref[...].astype(F32).reshape(BLK, W).astype(BF)
    out_ref[...] = dot(kront_ref[...], cols).reshape(NB, 8, W).astype(BF)


def forward(u_ref, block_ref, x_ref, gain_ref, bias_ref, weight_ref,
            mixed_ref, gate_ref, hidden_ref, act_ref, slope_ref):
    u = u_ref[...].astype(F32).reshape(BLK, W).astype(BF)
    mixed = dot(u, block_ref[...], TN)[:CS].astype(BF)
    mixed_ref[...] = mixed
    x = x_ref[...].astype(F32)
    gain = jnp.concatenate([gain_ref[...]] * 4, axis=1)
    bias = jnp.concatenate([bias_ref[...]] * 4, axis=1)
    gate = jax.nn.sigmoid(x * gain + bias)
    gate_ref[...] = gate
    hidden = (x + gate * mixed.astype(F32)).astype(BF)
    hidden_ref[...] = hidden
    pre = dot(weight_ref[0], hidden)
    root = 0.7978845608028654
    square = pre * pre
    curve = jnp.tanh(root * (pre + 0.044715 * (square * pre)))
    act_ref[...] = (pre * (0.5 * (1.0 + curve))).astype(BF)
    slope_ref[...] = 0.5 * (1.0 + curve) + pre * (0.5 * (1.0 - curve * curve)) * (
        root * (1.0 + (3 * 0.044715) * square)
    )


def channel(u_ref, block_ref, x_ref, gain_ref, weight_ref, mixed_ref, gate_ref, hidden_ref, act_ref,
            slope_ref, cot_ref, cots_ref, flag_ref, send_ref, rest_ref, factor_ref):
    q = flag_ref[0]
    act = act_ref[...].astype(F32)
    tiles = jnp.concatenate([cots_ref[g, CS:CS + 16, 0:HALF].astype(F32) for g in range(CB)], axis=0).astype(BF)
    k, m = iota((CS, HALF), 0), iota((CS, HALF), 1)
    start = KCH * (m // 16)
    low = dot(ones_where(k == start + m % 16), tiles)
    high = dot(ones_where((k == start + 16 + m % 16) & (m % 16 < 4)), tiles)
    second = jnp.where(m < 64, low + pltpu.roll(high, 64, 1), 0.0).astype(BF)
    pair, group = iota((HALF, HALF), 0), iota((HALF, HALF), 1)
    factor_ref[...] = dot(second, ones_where((pair == q * CB + group) & (group < CB)))
    back = dot(second, ones_where((pair == group * CB + q) & (group < CB)))
    d_act = jnp.zeros((CS, BLK), F32)
    grad_second = jnp.zeros((CS, HALF), F32)
    for g in range(CB):
        cot = cots_ref[g, 0:CS, :].astype(F32)
        d_act = d_act + back[:, g:g + 1] * cot
        column = jnp.sum(cot * act, axis=1, keepdims=True)
        grad_second = jnp.where(m == 32 + CB * g + q, column, grad_second)
    d_pre = (d_act.astype(BF).astype(F32) * slope_ref[...]).astype(BF)
    zeros = jnp.zeros((W - CS, BLK), F32)
    tall = jnp.concatenate([hidden_ref[...].astype(F32), zeros], axis=0).astype(BF)
    grad_first = dot(d_pre, tall, NT)
    d_hidden = cot_ref[...].astype(F32) + dot(weight_ref[0], d_pre, TN)
    gate = gate_ref[...]
    d_mixed = jnp.concatenate([d_hidden * gate, zeros], axis=0).astype(BF)
    d_gate = d_hidden * mixed_ref[...].astype(F32) * gate * (1.0 - gate)
    grad_gain = jnp.sum(d_gate * x_ref[...].astype(F32), axis=1, keepdims=True)
    grad_bias = jnp.sum(d_gate, axis=1, keepdims=True)
    gain = jnp.concatenate([gain_ref[...]] * 4, axis=1)
    rest_ref[...] = d_hidden + d_gate * gain
    v = dot(block_ref[...], d_mixed, NT)
    left, right = grad_first[:, :HALF], grad_first[:, HALF:]
    misc_b = jnp.where(m < 64, pltpu.roll(left, 32, 1), pltpu.roll(right, 64, 1))
    misc_b = jnp.where(m == 96, grad_gain, jnp.where(m == 97, grad_bias, misc_b))
    misc = jnp.concatenate([left, misc_b, grad_second, jnp.zeros((32, HALF), F32)], axis=0)
    right = jnp.where(iota((BLK, HALF), 1) < 32, v[:, HALF:], misc).reshape(NB, 8, HALF)
    left = v[:, :HALF].reshape(NB, 8, HALF)
    send_ref[:, 0:16, :] = jnp.concatenate([left, right], axis=1).astype(BF)
    u = u_ref[...].astype(F32).reshape(BLK, W).astype(BF)
    d_block = dot(u, d_mixed, NN)
    parts = [d_block[:, HALF * s:HALF * (s + 1)].reshape(NB, 8, HALF) for s in range(4)]
    send_ref[:, 16:48, :] = jnp.concatenate(parts, axis=1).astype(BF)


def cross_backward(recv_ref, x_ref, kron_ref, act_ref, send_ref, d_input_ref, misc_ref, pass_ref):
    pass_ref[...] = act_ref[...]
    head = recv_ref[:, 0:16, :].astype(F32)
    low = iota((NB, 8, HALF), 2) < 32
    left, right = head[:, 0:8, :], head[:, 8:16, :]
    v = jnp.concatenate(
        [left.reshape(BLK, HALF), jnp.where(low, right, 0.0).reshape(BLK, HALF)], axis=1
    ).astype(BF)
    misc = jnp.sum(right, axis=0)
    misc_ref[...] = misc
    d_input_ref[...] = dot(kron_ref[...], v).astype(BF)
    x = x_ref[...].astype(F32).reshape(BLK, W).astype(BF)
    pairs = dot(x, v, NT)
    same = iota((BLK, BLK), 0) % 8 == iota((BLK, BLK), 1) % 8
    rows = jnp.sum(jnp.where(same, pairs, 0.0).reshape(NB, 8, BLK), axis=1)
    high = rows.astype(BF)
    rest = (rows - high.astype(F32)).astype(BF)
    at, lane = iota((BLK, HALF), 0) // 8, iota((BLK, HALF), 1)
    cross = jnp.zeros((32, HALF), F32)
    for s in range(2):
        gather = ones_where(at == lane - 64 * s)
        cross = cross + dot(high[32 * s:32 * s + 32], gather) + dot(rest[32 * s:32 * s + 32], gather)
    tail = jnp.sum(recv_ref[:, 16:48, :].astype(F32), axis=0)
    send_ref[...] = jnp.concatenate([tail, cross, misc], axis=0)


def pack_last(recv_ref, own_ref, d_input_ref, flag_ref, send_ref):
    total = jnp.sum(recv_ref[...], axis=0)
    misc = jnp.where(flag_ref[3] > 0, total[64:72], own_ref[...])
    d_input = d_input_ref[...].astype(F32)
    left = d_input[:, :HALF].reshape(NB, 8, HALF)
    right = jnp.where(
        iota((NB, 8, HALF), 2) < 32, d_input[:, HALF:].reshape(NB, 8, HALF), misc[None]
    )
    send_ref[:, 0:16, :] = jnp.concatenate([left, right], axis=1).astype(BF)
    first = flag_ref[2] == 0
    block = jnp.where(first, total[0:16], total[16:32])
    cross = jnp.where(first, total[32:48], total[48:64])
    tail = jnp.concatenate([block, cross], axis=0).astype(BF)
    send_ref[:, 16:48, :] = jnp.broadcast_to(tail[None], (NB, 32, HALF))


def split_last(recv_ref, out_ref):
    recv = recv_ref[:, 16:32, :].astype(F32)
    left = recv[:, 0:8, :].reshape(BLK, HALF)
    right = recv[:, 8:16, :].reshape(BLK, HALF)
    out_ref[0:BLK, :] = jnp.concatenate([left, right], axis=1).astype(BF)
    cross = jnp.sum(recv_ref[:, 32:48, :].astype(F32), axis=0)
    out_ref[BLK:BLK + 16, :] = jnp.concatenate([cross, cross], axis=1).astype(BF)


def finish_output(hidden_ref, factor_ref, far_ref, out_ref, acts_ref, sems):
    copies = [pltpu.make_async_copy(far_ref.at[g], acts_ref.at[g], sems.at[g]) for g in range(CB)]
    for copy in copies:
        copy.start()
    factor = factor_ref[...]
    branch = jnp.zeros((CS, BLK), F32)
    for g in range(CB):
        copies[g].wait()
        branch = branch + factor[:, g:g + 1] * acts_ref[g].astype(F32)
    out_ref[...] = (hidden_ref[...].astype(F32) + branch.astype(BF).astype(F32)).astype(BF)


def finish_input(recv_ref, rest_ref, flag_ref, grad_ref, first_ref, second_ref, gain_ref, bias_ref):
    head = recv_ref[:, 0:16, :].astype(F32)
    left, misc = head[:, 0:8, :], head[:, 8:16, :].reshape(BLK, HALF)
    low = iota((BLK, HALF), 1) < 32
    d_input = jnp.concatenate([left.reshape(BLK, HALF), jnp.where(low, misc, 0.0)], axis=1)
    grad_ref[...] = (rest_ref[...] + d_input.T[:CS]).astype(BF)
    a, b = misc[0:CS], misc[CS:2 * CS]
    first_ref[0, :, 0:HALF] = jnp.where(iota((CS, HALF), 1) >= 32, a, pltpu.roll(b, 96, 1))
    first_ref[0, :, HALF:CS] = pltpu.roll(b, 64, 1)[:, 0:32]
    rows = misc[CS:CS + W].T
    gain_ref[...] = rows[96:97, 0:CS]
    bias_ref[...] = rows[97:98, 0:CS]
    pick = ones_where(iota((CS, KCH), 0) == iota((CS, KCH), 1) + KCH * flag_ref[0])
    second_ref[...] = dot(misc[2 * CS:3 * CS].astype(BF), pick, TN)[32:96]


def finish_sums(own_ref, swap_ref, flag_ref, block_ref, cross_ref):
    first = flag_ref[2] == 0
    own, swap = own_ref[...].astype(F32), swap_ref[...].astype(F32)
    low, high = jnp.where(first, own, swap), jnp.where(first, swap, own)
    block_ref[:, 0:W] = low[0:BLK]
    block_ref[:, W:BLK] = high[0:BLK]
    cross = jnp.concatenate([low[BLK:, 0:HALF], high[BLK:, 0:HALF]], axis=0)
    cross_ref[0:32, :] = cross[:, 0:64]
    cross_ref[32:64, :] = pltpu.roll(cross, 64, 1)[:, 0:64]


PAIR = [(i, i ^ 1) for i in range(CB)]


def on_device(layer_input, w_block, w_cross, ch_first, ch_second, gate_gain, gate_bias, cotangent):
    swap = functools.partial(lax.all_to_all, split_axis=0, concat_axis=0, tiled=True)
    ctx, ch = lax.axis_index("ctx"), lax.axis_index("ch")
    second_sum = (ctx >= 40) & (ctx < 60)
    flag = jnp.stack([ch, ch // 2, ch % 2, second_sum.astype(jnp.int32)]).astype(jnp.int32)
    xt, packed = call(
        begin, [((NB, 8, W), BF), ((CS + 16, BLK), BF)],
        layer_input, cotangent, ch_second.transpose(1, 2, 0).reshape(CB * CB, KCH),
        scratch=[pltpu.VMEM((CS, BLK), BF), pltpu.VMEM((CS, BLK), BF), pltpu.VMEM((24, HALF), F32),
                 pltpu.SemaphoreType.DMA((2,))],
        far=(0, 1), vmem=60,
    )
    x_cols = swap(xt, "ctx")
    cots = lax.all_gather(packed, "ch")
    gain, bias, kron, kront = call(
        prepare,
        [((CS, HALF), F32), ((CS, HALF), F32), ((BLK, BLK), BF), ((BLK, BLK), BF)],
        gate_gain.reshape(1, CS), gate_bias.reshape(1, CS), w_cross,
        scratch=[pltpu.VMEM((HALF, W), F32)],
    )
    (u_cols,) = call(cross_forward, [((NB, 8, W), BF)], kront, x_cols)
    u = swap(u_cols, "ctx")
    wide = (CS, BLK)
    mixed, gate, hidden, act, slope = call(
        forward, [(wide, BF), (wide, F32), (wide, BF), (wide, BF), (wide, F32)],
        u, w_block, layer_input, gain, bias, ch_first,
    )
    send, rest, factor = call(
        channel, [((NB, 48, HALF), BF), (wide, F32), ((CS, HALF), F32)],
        u, w_block, layer_input, gain, ch_first, mixed, gate, hidden, act, slope, cotangent, cots, flag,
        smem=(12,),
    )
    recv = swap(send, "ctx")
    send, d_input, misc, act = call(
        cross_backward,
        [((72, HALF), F32), ((BLK, W), BF), ((8, HALF), F32), ((CS, BLK), BF)],
        recv, x_cols, kron, act,
    )
    acts = lax.all_gather(act, "ch")
    (send,) = call(
        pack_last, [((NB, 48, HALF), BF)], lax.all_gather(send, "ch"), misc, d_input, flag, smem=(3,)
    )
    recv = swap(send, "ctx")
    (half,) = call(split_last, [((BLK + 16, W), BF)], recv)
    swapped = lax.ppermute(half, "ch", PAIR)
    grad_input, grad_first, grad_second, grad_gain, grad_bias = call(
        finish_input,
        [((CS, BLK), BF), ((1, CS, CS), F32), ((CB * CB, KCH), F32), ((1, CS), F32), ((1, CS), F32)],
        recv, rest, flag,
        smem=(2,),
    )
    (output,) = call(
        finish_output, [((CS, BLK), BF)], hidden, factor, acts,
        scratch=[pltpu.VMEM((CB, CS, BLK), BF), pltpu.SemaphoreType.DMA((CB,))],
        far=(2,), vmem=60, after=[half],
    )
    grad_block, grad_cross = call(
        finish_sums, [((BLK, BLK), F32), ((NB, NB), F32)], half, swapped, flag, smem=(2,)
    )
    return (
        output,
        grad_input,
        grad_block,
        grad_cross,
        grad_first,
        grad_second.reshape(CB, CB, KCH).transpose(2, 0, 1),
        grad_gain.reshape(CS),
        grad_bias.reshape(CS),
    )


def solution(mesh):
    in_specs = (
        P("ch", "ctx"),
        P(),
        P(),
        P("ch", None, None),
        P("ch", None, None),
        P("ch"),
        P("ch"),
        P("ch", "ctx"),
    )
    out_specs = (
        P("ch", "ctx"),
        P("ch", "ctx"),
        P(),
        P(),
        P("ch", None, None),
        P("ch", None, None),
        P("ch"),
        P("ch"),
    )
    return jax.shard_map(
        on_device, mesh=mesh, in_specs=in_specs, out_specs=out_specs, check_vma=False
    )
```
